32 devices in a mesh: dp: 8 (over z, x), tensor: 4 (over y, core).
Axes of the slice: x: 2, y: 2, z: 4, core: 2. Of those that a mesh axis runs over, the one named last changes fastest.
Arguments:
- tokens: bfloat16 [2, 8192, 768], P(None, ('dp', 'tensor')), may hold values from -6 to 6
- cotangent: bfloat16 [2, 8192, 768], P(None, ('dp', 'tensor')), may hold values from -6 to 6
- segment_ids: int32 [2, 16, 512], P(None, 'dp'), may hold values from 0 to 3, never falling along the last dimension, each value on 1 to 256 neighbouring positions
- qkv_weight: bfloat16 [2, 3, 768, 768], P(None, None, 'dp', 'tensor'), may hold values from -0.21875 to 0.21875
- out_weight: bfloat16 [2, 768, 768], P(None, 'tensor', 'dp'), may hold values from -0.875 to 0.875
- in_weight: bfloat16 [2, 768, 3072], P(None, 'dp', 'tensor'), may hold values from -0.21875 to 0.21875
- down_weight: bfloat16 [2, 3072, 768], P(None, 'tensor', 'dp'), may hold values from -0.109375 to 0.109375
- qv_bias: bfloat16 [2, 2, 12, 64], P(None, None, 'tensor', 'dp'), may hold values from -3 to 3
- in_bias: bfloat16 [2, 48, 64], P(None, 'tensor', 'dp'), may hold values from -3 to 3
- row_bias: bfloat16 [2, 2, 768], P(None, None, 'dp'), may hold values from -3 to 3
- norm_gain: bfloat16 [2, 2, 768], P(None, None, 'dp'), may hold values from 0.5 to 1.5
- norm_shift: bfloat16 [2, 2, 768], P(None, None, 'dp'), may hold values from -3 to 3
Outputs:
- output: float32 [2, 8192, 768], P(None, ('dp', 'tensor'))
- grad_tokens: float32 [2, 8192, 768], P(None, ('dp', 'tensor'))
- grad_qkv_weight: float32 [2, 3, 768, 768], P(None, None, 'dp', 'tensor')
- grad_out_weight: float32 [2, 768, 768], P(None, 'tensor', 'dp')
- grad_in_weight: float32 [2, 768, 3072], P(None, 'dp', 'tensor')
- grad_down_weight: float32 [2, 3072, 768], P(None, 'tensor', 'dp')
- grad_qv_bias: float32 [2, 2, 12, 64], P(None, None, 'tensor', 'dp')
- grad_in_bias: float32 [2, 48, 64], P(None, 'tensor', 'dp')
- grad_row_bias: float32 [2, 2, 768], P(None, None, 'dp')
- grad_norm_gain: float32 [2, 2, 768], P(None, None, 'dp')
- grad_norm_shift: float32 [2, 2, 768], P(None, None, 'dp')
The draws below stay inside these ranges and needn't reach their ends.
Inputs may be any that keep to these rules, and one draw needn't show every extreme that they name: `segment_ids`: within a packed row the ids never fall; a run of equal ids is one document of at most 256 tokens, and tokens attend only within their document.
All inputs are finite; a program needn't handle non-finite values.
Results may differ from the reference program's by a relative error of at most 0.03.
Values may be sent and summed in bfloat16 or wider, within the bound.
No kernel may reach another device: no remote copies, remote signals or barrier semaphores. Data moves between devices by JAX's collectives and lax.ppermute only.
A program may use at most 192 MiB of HBM per device.

```python
import math
import jax
import jax.numpy as jnp
import numpy as np
from jax import lax

D = 768
HEADS = 12
HD = 64
FF = 3072
LEN = 512
SEQ_MB = 2
MB = 2
LAYERS = 2
SEQS_MB = 16
TOK_MB = 8192
N_DP = 8


def raised(values, rng, source, target, parts, factor):
    def block_of(axis_at):
        return (jnp.arange(values.shape[axis_at]) // (values.shape[axis_at] // parts)).reshape((-1,) + (1,) * (values.ndim - 1 - axis_at))

    one_side = jax.random.permutation(rng, parts)[block_of(target)]
    far = (block_of(target) + parts // 2) % parts
    return jnp.where((block_of(source) == one_side) | (block_of(source) == far), factor * values, values)


def block_scale(key, shape, split, least, high):
    def one(dim, blocks):
        steps = jax.random.uniform(jax.random.fold_in(jax.random.fold_in(key, 6), dim), (blocks,), jnp.float32, least / len(split), high / len(split))
        return jnp.repeat(jnp.exp(steps), shape[dim] // blocks).reshape((-1,) + (1,) * (len(shape) - dim - 1))

    loudness = one(*split[0])
    for cut in split[1:]:
        loudness = loudness * one(*cut)
    return loudness


def split_up(amount, total, most, skew):
    loads = [(1 << 20) // math.isqrt(rank ** skew) + 1 for rank in range(2, amount + 1)]
    spare, given = total - most - (amount - 1), [1] * (amount - 1)
    while spare > 0:
        movable = [i for i in range(amount - 1) if given[i] < most]
        pool, left = sum([loads[i] for i in movable]), spare
        for i in movable:
            more = min(most - given[i], max(1, left * loads[i] // pool), spare)
            given[i] = given[i] + more
            spare = spare - more
    return np.array([most] + given)


def uneven(stream_key, number_of, total, reach, skew):
    if number_of == 2:
        one = jax.random.randint(stream_key, (), max(1, total - reach), min(reach, total - 1) + 1)
        return jnp.stack([one, total - one])
    sizes = jnp.asarray(split_up(number_of, total, reach, skew), jnp.int32)
    couples = (number_of - 1) // 2
    source_of, sink = sizes[1:1 + 2 * couples:2], sizes[2:2 + 2 * couples:2]
    room = jnp.minimum(source_of - 1, reach - sink)
    moved = jax.random.randint(jax.random.fold_in(stream_key, 1), (couples,), 0, 1 << 20) % (room + 1)
    sizes = sizes.at[1:1 + 2 * couples:2].set(source_of - moved).at[2:2 + 2 * couples:2].set(sink + moved)
    return sizes[jax.random.permutation(jax.random.fold_in(stream_key, 2), number_of)]


def centred(own_key, extent, scale, bound, split=(), kind=jnp.bfloat16):
    factor_of = block_scale(own_key, extent, split, -0.22, 0.18) if split else 1.0
    drawn = jax.random.normal(own_key, extent, jnp.float32) * scale * factor_of
    return jnp.minimum(jnp.maximum(drawn, -bound), bound).astype(kind)


def gaussian_with(key, dims, deviation, most, pieces, heavy, dtype=jnp.bfloat16):
    entries = deviation * jax.random.normal(key, dims, jnp.float32)
    if pieces:
        entries = entries * block_scale(key, dims, pieces, -0.22, 0.18)
    return jnp.clip(raised(entries, jax.random.fold_in(key, 3), *heavy), -most, most).astype(dtype)


def setup_inputs(seed: int = 0) -> dict:
    key_of = jax.random.split(jax.random.key(seed), 13)
    return {
        "tokens": centred(key_of[0], (MB, TOK_MB, D), 1.0, 6.0, ((1, 32),)),
        "cotangent": gaussian_with(key_of[1], (MB, TOK_MB, D), 1.0, 6.0, ((1, 32),), (1, 2, 32, 2.75)),
        "segment_ids": jax.vmap(lambda own: jnp.searchsorted(jnp.cumsum(uneven(own, 4, LEN, LEN // 2, 1)), jnp.arange(LEN), side="right"))(jax.random.split(key_of[2], MB * SEQS_MB)).reshape((MB, SEQS_MB, LEN)).astype(jnp.int32),
        "qkv_weight": centred(key_of[3], (LAYERS, 3, D, D), D ** -0.5, 0.21875, ((2, 8), (3, 4))),
        "out_weight": centred(key_of[4], (LAYERS, D, D), (D // 16) ** -0.5, 0.875, ((1, 4), (2, 8))),
        "in_weight": centred(key_of[5], (LAYERS, D, FF), D ** -0.5, 0.21875, ((1, 8), (2, 4))),
        "down_weight": centred(key_of[6], (LAYERS, FF, D), FF ** -0.5, 0.109375, ((1, 4), (2, 8))),
        "qv_bias": centred(key_of[7], (LAYERS, 2, HEADS, HD), 0.5, 3.0, ((2, 4), (3, 8))),
        "in_bias": centred(key_of[8], (LAYERS, FF // HD, HD), 0.5, 3.0, ((1, 4), (2, 8))),
        "row_bias": centred(key_of[9], (LAYERS, 2, D), 0.5, 3.0, ((2, 8),)),
        "norm_gain": jnp.clip(1.0 + 0.1 * jax.random.normal(key_of[10], (LAYERS, 2, D), jnp.float32), 0.5, 1.5).astype(jnp.bfloat16),
        "norm_shift": centred(key_of[11], (LAYERS, 2, D), 0.5, 3.0, ((2, 8),)),
    }


PRECISE = lax.Precision.HIGHEST
NORM_EPSILON = 1e-12
MASK_VALUE = -1000000000.0

@jax.custom_vjp
def low(v):
    return lax.optimization_barrier(v.astype(jnp.bfloat16)).astype(jnp.float32)

@jax.custom_vjp
def low_back(v):
    return v

def low_keep(v):
    return (low(v), None)

def low_pass(kept, grad):
    return (grad,)

def back_keep(v):
    return (v, None)

def back_low(kept, grad):
    return (low(grad),)
low.defvjp(low_keep, low_pass)
low_back.defvjp(back_keep, back_low)

def layer_norm(values, gain_row, shift_row):
    centre = values - lax.optimization_barrier(jnp.mean(values, axis=-1, keepdims=True))
    spread = lax.optimization_barrier(jnp.mean(centre * centre, axis=-1, keepdims=True))
    return centre * lax.rsqrt(spread + NORM_EPSILON) * gain_row + shift_row

def gelu_exact(values):
    return jax.nn.gelu(values, approximate=False)

def layer_forward(row_block, doc_ids, weights):
    qkv_weight, out_weight, in_weight, down_weight, qv_bias, in_bias, row_bias, norm_gain, norm_shift = weights
    score_scale = 1.0 / math.sqrt(HD)
    head_shape = (SEQ_MB, LEN, HEADS, HD)
    row_low = low(row_block)
    projected = jnp.einsum('rd,tdc->trc', row_low, qkv_weight, precision=PRECISE)
    queries = low_back(low(projected[0] + qv_bias[0].reshape(D)))
    key_rows = low_back(low(projected[1]))
    value_rows = low_back(low(projected[2] + qv_bias[1].reshape(D)))
    scores = jnp.einsum('sqhe,skhe->shqk', queries.reshape(head_shape), key_rows.reshape(head_shape), precision=PRECISE) * score_scale
    scores = low_back(scores)
    same_doc = doc_ids[:, None, :, None] == doc_ids[:, None, None, :]
    attention = low(jax.nn.softmax(jnp.where(same_doc, scores, MASK_VALUE), axis=-1))
    context = jnp.einsum('shqk,skhe->sqhe', attention, value_rows.reshape(head_shape), precision=PRECISE)
    context = low_back(low(context.reshape(SEQ_MB * LEN, D)))
    mixed_one = low_back(jnp.dot(context, out_weight, precision=PRECISE)) + row_bias[0] + row_block
    normed = layer_norm(mixed_one, norm_gain[0], norm_shift[0])
    hidden = low_back(jnp.dot(low(normed), in_weight, precision=PRECISE) + in_bias.reshape(FF))
    active = low(gelu_exact(hidden))
    mixed_two = low_back(jnp.dot(active, down_weight, precision=PRECISE)) + row_bias[1] + normed
    return layer_norm(mixed_two, norm_gain[1], norm_shift[1])

def reference(tokens, cotangent, segment_ids, qkv_weight, out_weight, in_weight, down_weight, qv_bias, in_bias, row_bias, norm_gain, norm_shift):
    weights = (qkv_weight.astype(jnp.float32), out_weight.astype(jnp.float32), in_weight.astype(jnp.float32), down_weight.astype(jnp.float32), qv_bias.astype(jnp.float32), in_bias.astype(jnp.float32), row_bias.astype(jnp.float32), norm_gain.astype(jnp.float32), norm_shift.astype(jnp.float32))
    blocks = MB * N_DP
    token_rows = tokens.astype(jnp.float32).reshape(blocks, SEQ_MB * LEN, D)
    cot_rows = cotangent.astype(jnp.float32).reshape(blocks, SEQ_MB * LEN, D)
    doc_blocks = segment_ids.reshape(blocks, SEQ_MB, LEN)

    def block_step(grad_totals, per_block):
        row_block, cot_block, doc_ids = per_block

        def whole_model(start_rows, model_weights):
            current = start_rows
            for layer_index in range(LAYERS):
                layer_weights = tuple((member[layer_index] for member in model_weights))
                current = layer_forward(current, doc_ids, layer_weights)
            return current
        result, pull_back = jax.vjp(whole_model, row_block, weights)
        grad_rows, grad_weights = pull_back(cot_block)
        return (jax.tree.map(jnp.add, grad_totals, grad_weights), (result, grad_rows))
    zero_grads = tuple((jnp.zeros_like(member) for member in weights))
    totals, (results, grad_inputs) = lax.scan(block_step, zero_grads, (token_rows, cot_rows, doc_blocks))
    return (results.reshape(MB, TOK_MB, D), grad_inputs.reshape(MB, TOK_MB, D), totals[0], totals[1], totals[2], totals[3], totals[4], totals[5], totals[6], totals[7], totals[8])
```

```python
from functools import partial

import jax
import jax.numpy as jnp
from jax import lax
from jax.experimental import pallas as pl
from jax.experimental.pallas import tpu as pltpu
from jax.sharding import PartitionSpec as P

HD = 64
NORM_EPSILON = 1e-12
MASK_VALUE = -1000000000.0
F32 = jnp.float32
BF16 = jnp.bfloat16
VMEM_BYTES = 48 * 1024 * 1024
ROOT_HALF = 0.7071067811865476
ROOT_TWO_PI = 0.3989422804014327


def dot_nn(left, right):
    return lax.dot_general(left, right, (((1,), (0,)), ((), ())), preferred_element_type=F32)


def dot_nt(left, right):
    return lax.dot_general(left, right, (((1,), (1,)), ((), ())), preferred_element_type=F32)


def normed_rows(values):
    centre = values - jnp.mean(values, axis=-1, keepdims=True)
    spread = jnp.mean(centre * centre, axis=-1, keepdims=True)
    scale = lax.rsqrt(spread + NORM_EPSILON)
    return centre * scale, scale


def norm_back(upstream, normal, scale, gain):
    grad = upstream * gain
    mean_grad = jnp.mean(grad, axis=-1, keepdims=True)
    mean_both = jnp.mean(grad * normal, axis=-1, keepdims=True)
    return scale * (grad - mean_grad - normal * mean_both)


def token_sums(upstream, normal, result):
    return jnp.concatenate(
        [
            jnp.sum(upstream * normal, axis=0, keepdims=True),
            jnp.sum(upstream, axis=0, keepdims=True),
            jnp.sum(result, axis=0, keepdims=True),
        ],
        axis=0,
    )


def turned(values):
    return values.astype(F32).T.astype(BF16)


def whole(shape):
    return pl.BlockSpec(shape, lambda t: (0,) * len(shape))


def slab(shape):
    return pl.BlockSpec((None,) + tuple(shape), lambda t: (t,) + (0,) * len(shape))


def shaped(shape, dtype):
    return jax.ShapeDtypeStruct(tuple(shape), dtype)


def call(body, name, steps, in_specs, out_specs, out_shape, scratch, flops, moved):
    return pl.pallas_call(
        body,
        grid=(steps,),
        in_specs=in_specs,
        out_specs=out_specs,
        out_shape=out_shape,
        scratch_shapes=scratch,
        compiler_params=pltpu.CompilerParams(
            dimension_semantics=("arbitrary",), vmem_limit_bytes=VMEM_BYTES
        ),
        cost_estimate=pl.CostEstimate(flops=flops, bytes_accessed=moved, transcendentals=0),
        name=name,
    )


def attend_kernel(
    x_ref, w_ref, qb_ref, vb_ref, vec_ref, doc_col_ref, doc_row_ref,
    qkv_ref, prob_ref, context_ref, normal_ref, scale_ref,
    low_ref, total_ref,
):
    step = pl.program_id(0)

    @pl.when(step == 0)
    def _():
        low_ref[...] = x_ref[...].astype(BF16)
        total_ref[...] = x_ref[...].astype(F32) + vec_ref[0:1]

    width = qb_ref.shape[-1]
    projected = dot_nn(low_ref[...], w_ref[:, : 3 * width])
    queries = ((projected[:, :width] + qb_ref[...]).astype(BF16)) * jnp.asarray(0.125, BF16)
    key_rows = projected[:, width : 2 * width].astype(BF16)
    value_full = projected[:, 2 * width :] + vb_ref[...]
    value_rows = value_full.astype(BF16)
    qkv_ref[:, :width] = queries
    qkv_ref[:, width : 2 * width] = key_rows
    qkv_ref[:, 2 * width :] = value_rows
    value_turned = turned(value_full)
    same_doc = doc_col_ref[...] == doc_row_ref[...]
    parts = []
    for head in range(width // HD):
        cols = slice(head * HD, (head + 1) * HD)
        scores = jnp.where(same_doc, dot_nt(key_rows[:, cols], queries[:, cols]), MASK_VALUE)
        expo = jnp.exp(scores - jnp.max(scores, axis=0, keepdims=True))
        weights = (expo * (1.0 / jnp.sum(expo, axis=0, keepdims=True))).astype(BF16)
        prob_ref[head] = weights
        parts.append(dot_nn(value_turned[cols], weights))
    context_turned = jnp.concatenate(parts, axis=0)
    context_ref[...] = context_turned.astype(BF16)
    context = context_turned.T.astype(BF16)
    total_ref[...] += dot_nt(context, w_ref[:, 3 * width :])

    @pl.when(step == pl.num_programs(0) - 1)
    def _():
        normal, scale = normed_rows(total_ref[...])
        normal_ref[...] = normal
        scale_ref[...] = scale


def attend(x, weight, q_bias, v_bias, vec, doc_ids):
    steps, width = q_bias.shape[0], q_bias.shape[2]
    rows, model = x.shape
    heads = width // HD
    return call(
        attend_kernel,
        "attend",
        steps,
        [
            whole((rows, model)),
            slab((model, 4 * width)),
            slab((1, width)),
            slab((1, width)),
            whole(vec.shape),
            whole((rows, 1)),
            whole((1, rows)),
        ],
        [
            slab((rows, 3 * width)),
            pl.BlockSpec((heads, rows, rows), lambda t: (t, 0, 0)),
            slab((width, rows)),
            whole((rows, model)),
            whole((rows, 1)),
        ],
        [
            shaped((steps, rows, 3 * width), BF16),
            shaped((steps * heads, rows, rows), BF16),
            shaped((steps, width, rows), BF16),
            shaped((rows, model), F32),
            shaped((rows, 1), F32),
        ],
        [pltpu.VMEM((rows, model), BF16), pltpu.VMEM((rows, model), F32)],
        2 * rows * model * 4 * width * steps + 4 * rows * rows * width * steps * 4,
        weight.size * 2 + steps * heads * rows * rows * 2,
    )(x, weight, q_bias, v_bias, vec, doc_ids.reshape(rows, 1), doc_ids.reshape(1, rows))


def hidden_kernel(normal_ref, vec_ref, w_ref, bias_ref, low_out_ref, active_ref, slope_ref, low_ref):
    @pl.when(pl.program_id(0) == 0)
    def _():
        low = (normal_ref[...] * vec_ref[1:2] + vec_ref[2:3]).astype(BF16)
        low_ref[...] = low
        low_out_ref[...] = low

    hidden = dot_nn(low_ref[...], w_ref[...]) + bias_ref[...]
    below = 0.5 + 0.5 * lax.erf(hidden * ROOT_HALF)
    active_ref[...] = (hidden * below).astype(BF16)
    slope_ref[...] = (below + hidden * (jnp.exp(hidden * hidden * -0.5) * ROOT_TWO_PI)).astype(BF16)


def hidden_units(normal, vec, weight, bias):
    steps, model, width = weight.shape
    rows = normal.shape[0]
    return call(
        hidden_kernel,
        "hidden",
        steps,
        [whole((rows, model)), whole(vec.shape), slab((model, width)), slab((1, width))],
        [whole((rows, model)), slab((rows, width)), slab((rows, width))],
        [
            shaped((rows, model), BF16),
            shaped((steps, rows, width), BF16),
            shaped((steps, rows, width), BF16),
        ],
        [pltpu.VMEM((rows, model), BF16)],
        2 * rows * model * width * steps * 2,
        weight.size * 2 + 4 * rows * width * steps,
    )(normal, vec, weight, bias)


def down_kernel(active_ref, w_ref, normal_ref, vec_ref, vec_two_ref, out_ref, normal_two_ref, scale_ref, total_ref):
    step = pl.program_id(0)

    @pl.when(step == 0)
    def _():
        total_ref[...] = normal_ref[...] * vec_ref[1:2] + vec_ref[2:3] + vec_two_ref[0:1]

    total_ref[...] += dot_nt(active_ref[...], w_ref[...])

    @pl.when(step == pl.num_programs(0) - 1)
    def _():
        normal, scale = normed_rows(total_ref[...])
        normal_two_ref[...] = normal
        scale_ref[...] = scale
        out_ref[...] = normal * vec_two_ref[1:2] + vec_two_ref[2:3]


def down(active, weight, normal, vec, vec_two):
    steps, rows, width = active.shape
    model = weight.shape[1]
    return call(
        down_kernel,
        "down",
        steps,
        [
            slab((rows, width)),
            slab((model, width)),
            whole((rows, model)),
            whole(vec.shape),
            whole(vec_two.shape),
        ],
        [whole((rows, model)), whole((rows, model)), whole((rows, 1))],
        [shaped((rows, model), F32), shaped((rows, model), F32), shaped((rows, 1), F32)],
        [pltpu.VMEM((rows, model), F32)],
        2 * rows * model * width * steps,
        weight.size * 2 + 2 * rows * width * steps + 12 * rows * model,
    )(active, weight, normal, vec, vec_two)


def down_back_kernel(
    up_ref, normal_ref, scale_ref, vec_ref, active_ref, slope_ref, w_ref,
    grad_w_ref, grad_hidden_ref, grad_rows_ref, sums_ref, unit_sums_ref,
    low_ref, turned_ref,
):
    @pl.when(pl.program_id(0) == 0)
    def _():
        upstream = up_ref[...].astype(F32)
        normal = normal_ref[...]
        grad = norm_back(upstream, normal, scale_ref[...], vec_ref[1:2])
        grad_rows_ref[...] = grad
        sums_ref[...] = token_sums(upstream, normal, grad)
        low_ref[...] = grad.astype(BF16)
        turned_ref[...] = grad.T.astype(BF16)

    grad_w_ref[...] = dot_nn(turned_ref[...], active_ref[...]).astype(BF16)
    grad_hidden = (dot_nn(low_ref[...], w_ref[...]) * slope_ref[...].astype(F32)).astype(BF16)
    grad_hidden_ref[...] = grad_hidden
    unit_sums_ref[...] = jnp.sum(grad_hidden.astype(F32), axis=0, keepdims=True)


def down_back(upstream, normal, scale, vec, active, slope, weight):
    steps, rows, width = active.shape
    model = weight.shape[1]
    return call(
        down_back_kernel,
        "down_back",
        steps,
        [
            whole((rows, model)),
            whole((rows, model)),
            whole((rows, 1)),
            whole(vec.shape),
            slab((rows, width)),
            slab((rows, width)),
            slab((model, width)),
        ],
        [
            slab((model, width)),
            slab((rows, width)),
            whole((rows, model)),
            whole((3, model)),
            slab((1, width)),
        ],
        [
            shaped((steps, model, width), BF16),
            shaped((steps, rows, width), BF16),
            shaped((rows, model), F32),
            shaped((3, model), F32),
            shaped((steps, 1, width), F32),
        ],
        [pltpu.VMEM((rows, model), BF16), pltpu.VMEM((model, rows), BF16)],
        4 * rows * model * width * steps,
        weight.size * 4 + 6 * rows * width * steps + 12 * rows * model,
    )(upstream, normal, scale, vec, active, slope, weight)


def hidden_back_kernel(
    low_in_ref, grad_hidden_ref, w_ref, grad_two_ref, normal_ref, scale_ref, vec_ref,
    grad_w_ref, grad_one_ref, sums_ref,
    turned_ref, total_ref,
):
    step = pl.program_id(0)

    @pl.when(step == 0)
    def _():
        turned_ref[...] = turned(low_in_ref[...])
        total_ref[...] = grad_two_ref[...]

    grad_w_ref[...] = dot_nn(turned_ref[...], grad_hidden_ref[...]).astype(BF16)
    total_ref[...] += dot_nt(grad_hidden_ref[...], w_ref[...])

    @pl.when(step == pl.num_programs(0) - 1)
    def _():
        upstream = total_ref[...]
        normal = normal_ref[...]
        grad = norm_back(upstream, normal, scale_ref[...], vec_ref[1:2])
        grad_one_ref[...] = grad
        sums_ref[...] = token_sums(upstream, normal, grad)


def hidden_back(low, grad_hidden, weight, grad_two, normal, scale, vec):
    steps, rows, width = grad_hidden.shape
    model = weight.shape[1]
    return call(
        hidden_back_kernel,
        "hidden_back",
        steps,
        [
            whole((rows, model)),
            slab((rows, width)),
            slab((model, width)),
            whole((rows, model)),
            whole((rows, model)),
            whole((rows, 1)),
            whole(vec.shape),
        ],
        [slab((model, width)), whole((rows, model)), whole((3, model))],
        [
            shaped((steps, model, width), BF16),
            shaped((rows, model), F32),
            shaped((3, model), F32),
        ],
        [pltpu.VMEM((model, rows), BF16), pltpu.VMEM((rows, model), F32)],
        4 * rows * model * width * steps,
        weight.size * 4 + 2 * rows * width * steps + 12 * rows * model,
    )(low, grad_hidden, weight, grad_two, normal, scale, vec)


def attend_back_kernel(
    x_ref, grad_one_ref, w_ref, qkv_ref, prob_ref, context_ref,
    grad_w_ref, grad_x_ref, sums_ref,
    low_ref, turned_ref, x_turned_ref,
):
    step = pl.program_id(0)

    @pl.when(step == 0)
    def _():
        grad = grad_one_ref[...]
        low_ref[...] = grad.astype(BF16)
        turned_ref[...] = grad.T.astype(BF16)
        x_turned_ref[...] = turned(x_ref[...].astype(BF16))
        grad_x_ref[...] = grad

    width = context_ref.shape[0]
    queries, key_rows = qkv_ref[:, :width], qkv_ref[:, width : 2 * width]
    value_rows = qkv_ref[:, 2 * width :]
    key_turned = turned(key_rows)
    grad_context = dot_nn(low_ref[...], w_ref[:, 3 * width :]).astype(BF16)
    grad_w_ref[:, 3 * width :] = dot_nt(turned_ref[...], context_ref[...]).astype(BF16)
    grad_q, grad_k, grad_v = [], [], []
    for head in range(width // HD):
        cols = slice(head * HD, (head + 1) * HD)
        low_weights = prob_ref[head]
        weights = low_weights.astype(F32)
        part = weights * dot_nt(value_rows[:, cols], grad_context[:, cols])
        centre = jnp.sum(part, axis=0, keepdims=True)
        grad_scores = (part - weights * centre).astype(BF16)
        grad_v.append(dot_nn(low_weights, grad_context[:, cols]))
        grad_k.append(dot_nn(grad_scores, queries[:, cols]))
        grad_q.append(dot_nn(key_turned[cols], grad_scores))
    stacked = jnp.concatenate(
        [(jnp.concatenate(grad_q, axis=0) * 0.125).T] + grad_k + grad_v, axis=1
    ).astype(BF16)
    grad_w_ref[:, : 3 * width] = dot_nn(x_turned_ref[...], stacked).astype(BF16)
    grad_x_ref[...] += dot_nt(stacked, w_ref[:, : 3 * width])
    sums_ref[...] = jnp.sum(stacked.astype(F32), axis=0, keepdims=True)


def attend_back(x, grad_one, weight, qkv, prob, context):
    steps, width, rows = context.shape
    model = weight.shape[1]
    heads = width // HD
    return call(
        attend_back_kernel,
        "attend_back",
        steps,
        [
            whole((rows, model)),
            whole((rows, model)),
            slab((model, 4 * width)),
            slab((rows, 3 * width)),
            pl.BlockSpec((heads, rows, rows), lambda t: (t, 0, 0)),
            slab((width, rows)),
        ],
        [slab((model, 4 * width)), whole((rows, model)), slab((1, 3 * width))],
        [
            shaped((steps, model, 4 * width), BF16),
            shaped((rows, model), F32),
            shaped((steps, 1, 3 * width), F32),
        ],
        [
            pltpu.VMEM((rows, model), BF16),
            pltpu.VMEM((model, rows), BF16),
            pltpu.VMEM((model, rows), BF16),
        ],
        4 * rows * model * 4 * width * steps + 8 * rows * rows * width * steps * 4,
        weight.size * 4 + steps * heads * rows * rows * 2 + 8 * rows * model,
    )(x, grad_one, weight, qkv, prob, context)


BOTH = ("tensor", "dp")


def swap_cores(values):
    count = lax.axis_size("tensor")
    return lax.ppermute(values, "tensor", [(i, i ^ 1) for i in range(count)])


def to_sequence(blocks, core):
    mine = lax.dynamic_index_in_dim(blocks, core, 0, keepdims=False)
    other = lax.dynamic_index_in_dim(blocks, 1 - core, 0, keepdims=False)
    got = swap_cores(other)
    return jnp.concatenate(
        [jnp.where(core == 0, mine, got), jnp.where(core == 0, got, mine)], axis=0
    )


def from_sequence(values, core):
    half = values.shape[0] // 2
    mine = lax.dynamic_slice_in_dim(values, core * half, half, 0)
    got = swap_cores(lax.dynamic_slice_in_dim(values, (1 - core) * half, half, 0))
    return jnp.stack([jnp.where(core == 0, mine, got), jnp.where(core == 0, got, mine)])


def gather_group(shard, teams):
    rows, width = shard.shape
    got = lax.all_gather(shard, BOTH, axis=0, tiled=True)
    return got.reshape(teams, -1, width)


def scatter_group(grads):
    return lax.psum_scatter(
        grads.reshape(-1, grads.shape[-1]), BOTH, scatter_dimension=0, tiled=True
    ).astype(F32)


def on_device(
    tokens, cotangent, segment_ids, qkv_weight, out_weight, in_weight, down_weight,
    qv_bias, in_bias, row_bias, norm_gain, norm_shift,
):
    teams, parts = lax.axis_size("tensor"), lax.axis_size("dp")
    layers, _, piece, width = qkv_weight.shape
    heads = width // HD
    model = piece * parts
    units = in_weight.shape[2]
    tensor_at = lax.axis_index("tensor")
    core = tensor_at % 2

    out_turned = jnp.swapaxes(out_weight, 1, 2)
    down_turned = jnp.swapaxes(down_weight, 1, 2)
    attn_shard = jnp.concatenate(
        [qkv_weight[:, 0], qkv_weight[:, 1], qkv_weight[:, 2], out_turned], axis=2
    )
    small = (qv_bias, in_bias, row_bias, norm_gain, norm_shift)
    lengths = [s.size for s in small]
    flat = jnp.concatenate([s.reshape(-1) for s in small]).reshape(1, -1)
    flat_all = lax.all_gather(flat, BOTH, axis=0, tiled=True).reshape(teams, parts, -1)
    edges = [0]
    for n in lengths:
        edges.append(edges[-1] + n)
    cut = [flat_all[:, :, a:b] for a, b in zip(edges[:-1], edges[1:])]
    qv_all = (
        cut[0].reshape((teams, parts) + qv_bias.shape).transpose(2, 3, 0, 4, 1, 5)
        .reshape(layers, 2, teams, 1, width).astype(F32)
    )
    in_all = (
        cut[1].reshape((teams, parts) + in_bias.shape).transpose(2, 0, 3, 1, 4)
        .reshape(layers, teams, 1, units).astype(F32)
    )
    vecs = jnp.stack(
        [
            c[0].reshape((parts,) + row_bias.shape).transpose(1, 2, 0, 3)
            .reshape(layers, 2, model).astype(F32)
            for c in cut[2:]
        ],
        axis=2,
    )

    weights = []
    for layer in range(layers):
        weights.append(
            [
                gather_group(attn_shard[layer], teams),
                gather_group(in_weight[layer], teams),
                gather_group(down_turned[layer], teams),
            ]
        )

    doc_ids = segment_ids[core, tensor_at // 2]
    current = to_sequence(tokens, core)
    upstream = to_sequence(cotangent, core)

    saved = []
    for layer in range(layers):
        attn_w, in_w, down_w = weights[layer]
        entered = current
        qkv, prob, context, normal_one, scale_one = attend(
            entered, attn_w, qv_all[layer, 0], qv_all[layer, 1], vecs[layer, 0], doc_ids
        )
        low, active, slope = hidden_units(normal_one, vecs[layer, 0], in_w, in_all[layer])
        current, normal_two, scale_two = down(
            active, down_w, normal_one, vecs[layer, 0], vecs[layer, 1]
        )
        saved.append(
            (entered, qkv, prob, context, normal_one, scale_one, low, active, slope, normal_two, scale_two)
        )
    output = from_sequence(current, core)

    grads = [None] * layers
    smalls = [None] * layers
    for layer in reversed(range(layers)):
        attn_w, in_w, down_w = weights[layer]
        (entered, qkv, prob, context, normal_one, scale_one, low, active, slope, normal_two, scale_two) = saved[layer]
        grad_down, grad_hidden, grad_two, sums_two, unit_sums = down_back(
            upstream, normal_two, scale_two, vecs[layer, 1], active, slope, down_w
        )
        grad_in, grad_one, sums_one = hidden_back(
            low, grad_hidden, in_w, grad_two, normal_one, scale_one, vecs[layer, 0]
        )
        grad_attn, upstream, qkv_sums = attend_back(entered, grad_one, attn_w, qkv, prob, context)
        grads[layer] = (
            scatter_group(grad_attn),
            scatter_group(grad_in),
            scatter_group(grad_down),
        )
        smalls[layer] = (qkv_sums, unit_sums, sums_one, sums_two)
    grad_tokens = from_sequence(upstream, core)

    sizes = [s.size for s in smalls[0]]
    flat = jnp.concatenate([s.reshape(-1) for layer in smalls for s in layer])
    flat = lax.psum(flat, BOTH).reshape(layers, -1)
    dp_at = lax.axis_index("dp")
    qkv_sums = flat[:, : sizes[0]].reshape(layers, teams, 3, heads, parts, -1)
    qkv_sums = lax.dynamic_index_in_dim(qkv_sums, tensor_at, 1, keepdims=False)
    qkv_sums = lax.dynamic_index_in_dim(qkv_sums, dp_at, 3, keepdims=False)
    grad_qv = jnp.stack([qkv_sums[:, 0], qkv_sums[:, 2]], axis=1)
    unit_sums = flat[:, sizes[0] : sizes[0] + sizes[1]].reshape(layers, teams, units // HD, parts, -1)
    unit_sums = lax.dynamic_index_in_dim(unit_sums, tensor_at, 1, keepdims=False)
    grad_unit = lax.dynamic_index_in_dim(unit_sums, dp_at, 2, keepdims=False)
    row_sums = flat[:, sizes[0] + sizes[1] :].reshape(layers, 2, 3, parts, piece)
    row_sums = lax.dynamic_index_in_dim(row_sums, dp_at, 3, keepdims=False)

    grad_attn = jnp.stack([g[0] for g in grads])
    grad_qkv = jnp.stack(
        [grad_attn[:, :, i * width : (i + 1) * width] for i in range(3)], axis=1
    )
    return (
        output,
        grad_tokens,
        grad_qkv,
        jnp.swapaxes(grad_attn[:, :, 3 * width :], 1, 2),
        jnp.stack([g[1] for g in grads]),
        jnp.swapaxes(jnp.stack([g[2] for g in grads]), 1, 2),
        grad_qv,
        grad_unit,
        row_sums[:, :, 2],
        row_sums[:, :, 0],
        row_sums[:, :, 1],
    )


def solution(mesh):
    placed = (
        P(None, ("dp", "tensor"), None),
        P(None, ("dp", "tensor"), None),
        P(None, "dp", None),
        P(None, None, "dp", "tensor"),
        P(None, "tensor", "dp"),
        P(None, "dp", "tensor"),
        P(None, "tensor", "dp"),
        P(None, None, "tensor", "dp"),
        P(None, "tensor", "dp"),
        P(None, None, "dp"),
        P(None, None, "dp"),
        P(None, None, "dp"),
    )
    return jax.shard_map(
        on_device,
        mesh=mesh,
        in_specs=placed,
        out_specs=(
            P(None, ("dp", "tensor"), None),
            P(None, ("dp", "tensor"), None),
            P(None, None, "dp", "tensor"),
            P(None, "tensor", "dp"),
            P(None, "dp", "tensor"),
            P(None, "tensor", "dp"),
            P(None, None, "tensor", "dp"),
            P(None, "tensor", "dp"),
            P(None, None, "dp"),
            P(None, None, "dp"),
            P(None, None, "dp"),
        ),
        check_vma=False,
    )
```

```python
from functools import partial

import jax
import jax.numpy as jnp
from jax import lax
from jax.experimental import pallas as pl
from jax.experimental.pallas import tpu as pltpu
from jax.sharding import PartitionSpec as P

HD = 64
NORM_EPSILON = 1e-12
MASK_VALUE = -1000000000.0
F32 = jnp.float32
BF16 = jnp.bfloat16
STREAM_BYTES = 60 * 1024 * 1024
MERGE_BYTES = 32 * 1024 * 1024
FORWARD_SCALE, BACKWARD_SCALE = 0.25, 2000


def lasting(microseconds, scale):
    return pl.CostEstimate(flops=int(1.15e9 * microseconds * scale), bytes_accessed=0, transcendentals=0)


ROOT_HALF = 0.7071067811865476
ROOT_TWO_PI = 0.3989422804014327

LINE = (1, 3, 0, 2)

GATHERED = (1,)
SCATTERED = ((1, 1),)


def dot_nn(left, right):
    return lax.dot_general(left, right, (((1,), (0,)), ((), ())), preferred_element_type=F32)


def dot_nt(left, right):
    return lax.dot_general(left, right, (((1,), (1,)), ((), ())), preferred_element_type=F32)


def dot_tn(left, right):
    return lax.dot_general(left, right, (((0,), (0,)), ((), ())), preferred_element_type=F32)


def normed_rows(values):
    centre = values - jnp.mean(values, axis=-1, keepdims=True)
    spread = jnp.mean(centre * centre, axis=-1, keepdims=True)
    scale = lax.rsqrt(spread + NORM_EPSILON)
    return centre * scale, scale


def norm_back(upstream, normal, scale, gain):
    grad = upstream * gain
    mean_grad = jnp.mean(grad, axis=-1, keepdims=True)
    mean_both = jnp.mean(grad * normal, axis=-1, keepdims=True)
    return scale * (grad - mean_grad - normal * mean_both)


def token_sums(upstream, normal, result):
    return jnp.concatenate(
        [
            jnp.sum(upstream * normal, axis=0, keepdims=True),
            jnp.sum(upstream, axis=0, keepdims=True),
            jnp.sum(result, axis=0, keepdims=True),
        ],
        axis=0,
    )


def turned(values):
    return values.astype(F32).T.astype(BF16)


ANYWHERE = pl.BlockSpec(memory_space=pl.ANY)
IN_VMEM = pl.BlockSpec(memory_space=pltpu.VMEM)
IN_SMEM = pl.BlockSpec(memory_space=pltpu.SMEM)


def shaped(shape, dtype):
    return jax.ShapeDtypeStruct(tuple(shape), dtype)


class Rows:
    def __init__(self, array, split=False):
        self.operands = [array]
        self.scratch = [
            pltpu.VMEM(array.shape, array.dtype),
            pltpu.SemaphoreType.DMA((array.shape[0] if split else 1,)),
        ]

    def bind(self, refs, scratch, table):
        (self.ref,), (self.held, self.sems) = refs, scratch
        return self

    def copy(self, index):
        if index is None:
            return pltpu.make_async_copy(self.ref, self.held, self.sems.at[0])
        return pltpu.make_async_copy(self.ref.at[index], self.held.at[index], self.sems.at[index])

    def start(self, index=None):
        self.copy(index).start()

    def wait(self, index=None):
        self.copy(index).wait()


class Weights:
    def __init__(self, group, start, width):
        self.group, self.cols = group, pl.ds(group.start + start, width)
        self.operands = list(group.arrays)
        model = group.model
        self.scratch = [
            pltpu.VMEM((len(LINE), model, width), BF16),
            pltpu.SemaphoreType.DMA((len(LINE), len(group.places) if group.common else 1)),
        ]

    def bind(self, refs, scratch, table):
        self.refs, (self.held, self.sems), self.table = refs, scratch, table
        return self

    def copies(self, index):
        if not self.group.common:
            yield pltpu.make_async_copy(
                self.refs[index].at[:, self.cols], self.held.at[index], self.sems.at[index, 0]
            )
            return
        places = len(self.group.places)
        piece = self.group.model // places
        for place in range(places):
            row = pl.multiple_of(self.table[index] + self.table[len(LINE) + place], piece)
            yield pltpu.make_async_copy(
                self.refs[0].at[pl.ds(row, piece), self.cols],
                self.held.at[index, pl.ds(place * piece, piece)],
                self.sems.at[index, place],
            )

    def start(self, index):
        for copy in self.copies(index):
            copy.start()

    def wait(self, index):
        for copy in self.copies(index):
            copy.wait()


class Result:
    def __init__(self, shape, dtype, split=False):
        self.shapes = [shaped(shape, dtype)]
        self.indices = range(shape[0]) if split else (None,)
        self.scratch = [
            pltpu.VMEM(shape, dtype),
            pltpu.SemaphoreType.DMA((shape[0] if split else 1,)),
        ]

    def bind(self, refs, scratch, table):
        (self.ref,), (self.held, self.sems) = refs, scratch
        return self

    def copy(self, index):
        if index is None:
            return pltpu.make_async_copy(self.held, self.ref, self.sems.at[0])
        return pltpu.make_async_copy(self.held.at[index], self.ref.at[index], self.sems.at[index])

    def start(self, index=None):
        self.copy(index).start()

    def finish(self):
        for index in self.indices:
            self.copy(index).wait()


class Grads:
    def __init__(self, model, width, places, common):
        self.model, self.places, self.common = model, places, common
        teams = len(LINE)
        if common:
            self.shapes = [shaped((teams * model, width), BF16)]
        else:
            self.shapes = [shaped((2, model, width), BF16)] * 2
        self.scratch = [
            pltpu.VMEM((teams, model, width), BF16),
            pltpu.SemaphoreType.DMA((teams, len(places) if common else 1)),
        ]

    def bind(self, refs, scratch, table):
        self.refs, (self.held, self.sems), self.table = refs, scratch, table
        return self

    def copies(self, index):
        if not self.common:
            yield pltpu.make_async_copy(
                self.held.at[index], self.refs[index // 2].at[index % 2], self.sems.at[index, 0]
            )
            return
        places = len(self.places)
        piece = self.model // places
        for place in range(places):
            row = pl.multiple_of(self.table[index] + self.table[len(LINE) + place], piece)
            yield pltpu.make_async_copy(
                self.held.at[index, pl.ds(place * piece, piece)],
                self.refs[0].at[pl.ds(row, piece)],
                self.sems.at[index, place],
            )

    def start(self, index):
        for copy in self.copies(index):
            copy.start()

    def finish(self):
        for index in range(len(LINE)):
            for copy in self.copies(index):
                copy.wait()


def streamed(body, name, table, ins, outs, scratch=(), after=(), lasts=15, scale=FORWARD_SCALE):
    waits = len(after)
    operands = [array for item in ins for array in item.operands]
    shapes = [shape for item in outs for shape in item.shapes]

    def wrapped(*refs):
        refs = list(refs)

        def take(count):
            taken = refs[:count]
            del refs[:count]
            return taken

        (table_ref,) = take(1)
        in_refs = [take(len(item.operands)) for item in ins]
        take(waits)
        out_refs = [take(len(item.shapes)) for item in outs]
        (token_ref,) = take(1)
        token_ref[...] = jnp.zeros((8, 128), F32)
        inlets = [item.bind(own, take(len(item.scratch)), table_ref) for item, own in zip(ins, in_refs)]
        outlets = [item.bind(own, take(len(item.scratch)), table_ref) for item, own in zip(outs, out_refs)]
        body(inlets, outlets, *refs)
        for outlet in outlets:
            outlet.finish()

    kernel = pl.pallas_call(
        wrapped,
        in_specs=[IN_SMEM] + [ANYWHERE] * (len(operands) + waits),
        out_specs=[ANYWHERE] * len(shapes) + [IN_VMEM],
        out_shape=shapes + [shaped((8, 128), F32)],
        scratch_shapes=[entry for item in list(ins) + list(outs) for entry in item.scratch] + list(scratch),
        compiler_params=pltpu.CompilerParams(vmem_limit_bytes=STREAM_BYTES),
        cost_estimate=lasting(lasts, scale),
        name=name,
    )
    return kernel(table, *operands, *after)


def attend_body(inlets, outlets, low_ref):
    x, doc_col, doc_row, vec, q_bias, v_bias, weights = inlets
    qkv, prob, context, normal_out, scale_out = outlets
    steps, _, width = q_bias.held.shape
    heads = width // HD
    for inlet in (doc_col, doc_row, vec, q_bias, v_bias, x):
        inlet.start()
    weights.start(0)
    weights.start(1)
    for inlet in (doc_col, doc_row, vec, q_bias, v_bias, x):
        inlet.wait()
    low_ref[...] = x.held[...].astype(BF16)
    total = x.held[...].astype(F32) + vec.held[0:1]
    same_doc = doc_col.held[...] == doc_row.held[...]
    for step in range(steps):
        weights.wait(step)
        if step + 2 < steps:
            weights.start(step + 2)
        projected = dot_nn(low_ref[...], weights.held[step, :, : 3 * width])
        queries = (projected[:, :width] + q_bias.held[step]).astype(BF16) * jnp.asarray(0.125, BF16)
        key_rows = projected[:, width : 2 * width].astype(BF16)
        value_full = projected[:, 2 * width :] + v_bias.held[step]
        qkv.held[step, :, :width] = queries
        qkv.held[step, :, width : 2 * width] = key_rows
        qkv.held[step, :, 2 * width :] = value_full.astype(BF16)
        qkv.start(step)
        value_turned = turned(value_full)
        parts = []
        for head in range(heads):
            cols = slice(head * HD, (head + 1) * HD)
            scores = jnp.where(same_doc, dot_nt(key_rows[:, cols], queries[:, cols]), MASK_VALUE)
            expo = jnp.exp(scores - jnp.max(scores, axis=0, keepdims=True))
            chances = (expo * (1.0 / jnp.sum(expo, axis=0, keepdims=True))).astype(BF16)
            prob.held[step * heads + head] = chances
            prob.start(step * heads + head)
            parts.append(dot_nn(value_turned[cols], chances))
        context_turned = jnp.concatenate(parts, axis=0)
        context.held[step] = context_turned.astype(BF16)
        context.start(step)
        total = total + dot_nt(context_turned.T.astype(BF16), weights.held[step, :, 3 * width :])
    normal, scale = normed_rows(total)
    normal_out.held[...] = normal
    scale_out.held[...] = scale
    normal_out.start()
    scale_out.start()


def attend(table, x, weights, q_bias, v_bias, vec, doc_ids, after=()):
    steps, width = q_bias.shape[0], q_bias.shape[2]
    rows, model = x.shape
    heads = width // HD
    return streamed(
        attend_body,
        "attend",
        table,
        [
            Rows(x), Rows(doc_ids.reshape(rows, 1)), Rows(doc_ids.reshape(1, rows)), Rows(vec), Rows(q_bias),
            Rows(v_bias), Weights(weights, 0, 4 * width),
        ],
        [
            Result((steps, rows, 3 * width), BF16, True),
            Result((steps * heads, rows, rows), BF16, True),
            Result((steps, width, rows), BF16, True),
            Result((rows, model), F32),
            Result((rows, 1), F32),
        ],
        [pltpu.VMEM((rows, model), BF16)],
        after=after,
    )


def forward_body(inlets, outlets, low_ref):
    normal, vec, vec_two, bias, first, second = inlets
    low_out, active, slope, out, normal_two, scale_two = outlets
    steps = bias.held.shape[0]
    for inlet in (vec, vec_two, bias, normal):
        inlet.start()
    for step in range(2):
        first.start(step)
        second.start(step)
    for inlet in (vec, vec_two, bias, normal):
        inlet.wait()
    rows = normal.held[...] * vec.held[1:2] + vec.held[2:3]
    low_ref[...] = rows.astype(BF16)
    low_out.held[...] = rows.astype(BF16)
    low_out.start()
    total = rows + vec_two.held[0:1]
    for step in range(steps):
        first.wait(step)
        second.wait(step)
        if step + 2 < steps:
            first.start(step + 2)
            second.start(step + 2)
        hidden = dot_nn(low_ref[...], first.held[step]) + bias.held[step]
        below = 0.5 + 0.5 * lax.erf(hidden * ROOT_HALF)
        value = (hidden * below).astype(BF16)
        active.held[step] = value
        slope.held[step] = (below + hidden * (jnp.exp(hidden * hidden * -0.5) * ROOT_TWO_PI)).astype(BF16)
        active.start(step)
        slope.start(step)
        total = total + dot_nt(value, second.held[step])
    normal_value, scale = normed_rows(total)
    normal_two.held[...] = normal_value
    scale_two.held[...] = scale
    out.held[...] = normal_value * vec_two.held[1:2] + vec_two.held[2:3]
    for outlet in (normal_two, scale_two, out):
        outlet.start()


def forward(table, normal, vec, vec_two, bias, first, second, after=()):
    steps, _, width = bias.shape
    rows, model = normal.shape
    return streamed(
        forward_body,
        "forward",
        table,
        [
            Rows(normal), Rows(vec), Rows(vec_two), Rows(bias),
            Weights(first, 0, width), Weights(second, 0, width),
        ],
        [
            Result((rows, model), BF16),
            Result((steps, rows, width), BF16, True),
            Result((steps, rows, width), BF16, True),
            Result((rows, model), F32),
            Result((rows, model), F32),
            Result((rows, 1), F32),
        ],
        [pltpu.VMEM((rows, model), BF16)],
        after=after,
    )


def forward_back_body(inlets, outlets, low_two_ref):
    up, normal_two, scale_two, vec_two, active, slope, second, first, low, normal, scale, vec = inlets
    grads, grad_one, sums_two, sums_one, unit_sums = outlets
    steps, _, width = active.held.shape
    for inlet in (scale_two, vec_two, up, normal_two):
        inlet.start()
    for inlet in (scale_two, vec_two, up, normal_two):
        inlet.wait()

    def bring(step):
        for inlet in (active, second, slope, first):
            inlet.start(step)

    bring(0)
    low.start()
    bring(1)
    upstream, normal_value = up.held[...].astype(F32), normal_two.held[...]
    grad = norm_back(upstream, normal_value, scale_two.held[...], vec_two.held[1:2])
    low_two_ref[...] = grad.astype(BF16)
    total = grad
    sums_two.held[...] = token_sums(upstream, normal_value, grad)
    sums_two.start()
    for step in range(steps):
        for inlet in (active, second, slope, first):
            inlet.wait(step)
        if step == 0:
            low.wait()
        if step + 2 < steps:
            bring(step + 2)
        elif step + 2 == steps:
            for inlet in (scale, vec, normal):
                inlet.start()
        grads.held[step, :, width:] = dot_tn(low_two_ref[...], active.held[step]).astype(BF16)
        value = (dot_nn(low_two_ref[...], second.held[step]) * slope.held[step].astype(F32)).astype(BF16)
        unit_sums.held[step] = jnp.sum(value.astype(F32), axis=0, keepdims=True)
        grads.held[step, :, :width] = dot_tn(low.held[...], value).astype(BF16)
        grads.start(step)
        unit_sums.start(step)
        total = total + dot_nt(value, first.held[step])
    for inlet in (scale, vec, normal):
        inlet.wait()
    normal_value = normal.held[...]
    grad = norm_back(total, normal_value, scale.held[...], vec.held[1:2])
    grad_one.held[...] = grad
    sums_one.held[...] = token_sums(total, normal_value, grad)
    grad_one.start()
    sums_one.start()


def forward_back(
    table, upstream, normal_two, scale_two, vec_two, active, slope, first, second, low, normal, scale, vec, common,
    after=(),
):
    steps, rows, width = active.shape
    model = low.shape[1]
    return streamed(
        forward_back_body,
        "forward_back",
        table,
        [
            Rows(upstream), Rows(normal_two), Rows(scale_two), Rows(vec_two), Rows(active, True), Rows(slope, True),
            Weights(second, 0, width), Weights(first, 0, width), Rows(low), Rows(normal), Rows(scale), Rows(vec),
        ],
        [
            Grads(model, 2 * width, first.places, common),
            Result((rows, model), F32),
            Result((3, model), F32),
            Result((3, model), F32),
            Result((steps, 1, width), F32, True),
        ],
        [pltpu.VMEM((rows, model), BF16)],
        after=after,
        lasts=19,
        scale=BACKWARD_SCALE,
    )


def attend_back_body(inlets, outlets, low_ref, x_low_ref):
    x, grad_one, qkv, prob, context, weights = inlets
    grads, grad_x, sums = outlets
    steps, width, _ = context.held.shape
    heads = prob.held.shape[0] // steps

    def bring(step):
        weights.start(step)
        qkv.start(step)
        for head in range(heads):
            prob.start(step * heads + head)
        context.start(step)

    grad_one.start()
    bring(0)
    x.start()
    bring(1)
    grad_one.wait()
    low_ref[...] = grad_one.held[...].astype(BF16)
    total = grad_one.held[...]
    for step in range(steps):
        weights.wait(step)
        qkv.wait(step)
        context.wait(step)
        for head in range(heads):
            prob.wait(step * heads + head)
        if step == 0:
            x.wait()
            x_low_ref[...] = x.held[...].astype(BF16)
        if step + 2 < steps:
            bring(step + 2)
        block = qkv.held[step]
        queries, key_rows = block[:, :width], block[:, width : 2 * width]
        value_rows = block[:, 2 * width :]
        key_turned = turned(key_rows)
        grad_context = dot_nn(low_ref[...], weights.held[step, :, 3 * width :]).astype(BF16)
        grad_q, grad_k, grad_v = [], [], []
        for head in range(heads):
            cols = slice(head * HD, (head + 1) * HD)
            low_weights = prob.held[step * heads + head]
            chances = low_weights.astype(F32)
            part = chances * dot_nt(value_rows[:, cols], grad_context[:, cols])
            centre = jnp.sum(part, axis=0, keepdims=True)
            grad_scores = (part - chances * centre).astype(BF16)
            grad_v.append(dot_nn(low_weights, grad_context[:, cols]))
            grad_k.append(dot_nn(grad_scores, queries[:, cols]))
            grad_q.append(dot_nn(key_turned[cols], grad_scores))
        stacked = jnp.concatenate(
            [(jnp.concatenate(grad_q, axis=0) * 0.125).T] + grad_k + grad_v, axis=1
        ).astype(BF16)
        grads.held[step, :, : 3 * width] = dot_tn(x_low_ref[...], stacked).astype(BF16)
        grads.held[step, :, 3 * width :] = dot_tn(low_ref[...], turned(context.held[step])).astype(BF16)
        grads.start(step)
        total = total + dot_nt(stacked, weights.held[step, :, : 3 * width])
        sums.held[step] = jnp.sum(stacked.astype(F32), axis=0, keepdims=True)
        sums.start(step)
    grad_x.held[...] = total
    grad_x.start()


def attend_back(table, x, grad_one, weights, qkv, prob, context, common, after=()):
    steps, width, rows = context.shape
    model = x.shape[1]
    return streamed(
        attend_back_body,
        "attend_back",
        table,
        [
            Rows(x), Rows(grad_one), Rows(qkv, True), Rows(prob, True), Rows(context, True),
            Weights(weights, 0, 4 * width),
        ],
        [
            Grads(model, 4 * width, weights.places, common),
            Result((rows, model), F32),
            Result((steps, 1, 3 * width), F32, True),
        ],
        [pltpu.VMEM((rows, model), BF16), pltpu.VMEM((rows, model), BF16)],
        after=after,
        lasts=22,
        scale=BACKWARD_SCALE,
    )


def whole(shape):
    return pl.BlockSpec(shape, lambda t: (0,) * len(shape))


def call(body, name, steps, in_specs, out_specs, out_shape, scratch, flops, moved, after=(), token=False):
    single = not isinstance(out_shape, list)
    out_specs = [out_specs] if single else list(out_specs)
    out_shape = [out_shape] if single else list(out_shape)
    inputs, outputs, waits = len(in_specs), len(out_shape), len(after)
    if token:
        out_specs.append(whole((8, 128)))
        out_shape.append(shaped((8, 128), F32))

    def wrapped(*refs):
        made = refs[inputs + waits :]
        if token:
            made[outputs][...] = jnp.zeros((8, 128), F32)
        body(*refs[:inputs], *made[:outputs], *made[outputs + token :])

    kernel = pl.pallas_call(
        wrapped,
        grid=(steps,),
        in_specs=list(in_specs) + [ANYWHERE] * waits,
        out_specs=out_specs,
        out_shape=out_shape,
        scratch_shapes=scratch,
        compiler_params=pltpu.CompilerParams(
            dimension_semantics=("arbitrary",), vmem_limit_bytes=MERGE_BYTES
        ),
        cost_estimate=lasting(2, BACKWARD_SCALE),
        name=name,
    )

    def run(*args):
        made = kernel(*args, *after)
        if not single or token:
            return made
        return made[0]

    return run


def reorder_kernel(values_ref, place_ref, out_ref):
    values = values_ref[...]
    high = values.astype(BF16)
    low = (values - high.astype(F32)).astype(BF16)
    place = place_ref[...]
    out_ref[...] = dot_nt(high, place) + dot_nt(low, place)


def reorder(values, place, after=()):
    rows, model = values.shape
    return call(
        reorder_kernel,
        "reorder",
        1,
        [whole((rows, model)), whole((model, model))],
        whole((rows, model)),
        shaped((rows, model), F32),
        [],
        4 * rows * model * model,
        8 * rows * model,
        after=after,
    )(values, place)


def dp_bits(parts):
    return list(range(1, parts.bit_length() - 1)) + [0]


def dp_places(parts):
    bits = dp_bits(parts)
    return [sum(((place >> k) & 1) << bit for k, bit in enumerate(bits)) for place in range(parts)]


def trade(values, axis, bit):
    return lax.ppermute(values, axis, [(i, i ^ (1 << bit)) for i in range(lax.axis_size(axis))])


def swap_cores(values):
    return trade(values, "tensor", 0)


def to_sequence(blocks, core):
    mine = lax.dynamic_index_in_dim(blocks, core, 0, keepdims=False)
    other = lax.dynamic_index_in_dim(blocks, 1 - core, 0, keepdims=False)
    got = swap_cores(other)
    return jnp.concatenate(
        [jnp.where(core == 0, mine, got), jnp.where(core == 0, got, mine)], axis=0
    )


def from_sequence(values, core):
    half = values.shape[0] // 2
    mine = lax.dynamic_slice_in_dim(values, core * half, half, 0)
    got = swap_cores(lax.dynamic_slice_in_dim(values, (1 - core) * half, half, 0))
    return jnp.stack([jnp.where(core == 0, mine, got), jnp.where(core == 0, got, mine)])


def joined(*blocks):
    return jnp.concatenate(blocks, axis=0)


def gated(values, token):
    return values if token is None else values + token[0, 0].astype(values.dtype)


class Group:
    def __init__(self, arrays, model, places, common):
        self.arrays, self.model, self.places, self.common = arrays, model, places, common
        self.start = 0


def mark(*arrays):
    def body(*refs):
        refs[-1][...] = jnp.zeros((8, 128), F32)

    return pl.pallas_call(
        body,
        in_specs=[ANYWHERE] * len(arrays),
        out_specs=IN_VMEM,
        out_shape=shaped((8, 128), F32),
        cost_estimate=lasting(0.5, FORWARD_SCALE),
        name="mark",
    )(*arrays)


def moved(plan, after):
    arrays = []
    for parts in plan:
        for array, _, _ in parts:
            if not any(array is other for other in arrays):
                arrays.append(array)
    steps = []
    for out, parts in enumerate(plan):
        at = 0
        for array, start, rows in parts:
            source = [array is other for other in arrays].index(True)
            steps.append((source, start, out, at, rows))
            at += rows
    shapes = [
        shaped((sum(rows for _, _, rows in parts),) + parts[0][0].shape[1:], parts[0][0].dtype) for parts in plan
    ]
    count, waits = len(arrays), len(after)

    def body(*refs):
        refs = list(refs)
        sources, results = refs[:count], refs[count + waits : count + waits + len(plan)]
        token_ref, *held = refs[count + waits + len(plan) : -2]
        sems, out_sems = refs[-2:]
        token_ref[...] = jnp.zeros((8, 128), F32)
        brought = [
            pltpu.make_async_copy(
                sources[source].at[pl.ds(start, rows)], held[out].at[pl.ds(at, rows)], sems.at[k]
            )
            for k, (source, start, out, at, rows) in enumerate(steps)
        ]
        for copy in brought:
            copy.start()
        for copy in brought:
            copy.wait()
        given = [pltpu.make_async_copy(held[k], results[k], out_sems.at[k]) for k in range(len(plan))]
        for copy in given:
            copy.start()
        for copy in given:
            copy.wait()

    return pl.pallas_call(
        body,
        in_specs=[ANYWHERE] * (count + waits),
        out_specs=[ANYWHERE] * len(shapes) + [IN_VMEM],
        out_shape=shapes + [shaped((8, 128), F32)],
        scratch_shapes=[pltpu.VMEM(shape.shape, shape.dtype) for shape in shapes]
        + [pltpu.SemaphoreType.DMA((len(steps),)), pltpu.SemaphoreType.DMA((len(plan),))],
        compiler_params=pltpu.CompilerParams(vmem_limit_bytes=MERGE_BYTES),
        cost_estimate=lasting(2, FORWARD_SCALE),
        name="moved",
    )(*arrays, *after)


def built(plan, after, fine):
    if fine:
        *made, token = moved(plan, after)
        return made, token
    token = mark(*after) if after else None
    made = [joined(*[gated(array[start : start + rows], token) for array, start, rows in parts]) for parts in plan]
    return made, mark(*made)


def gather_group(shard, places):
    parts = len(places)
    bits = dp_bits(parts)
    fine = shard.shape[0] % 16 == 0
    block = shard
    for bit in bits[:-1]:
        got = trade(block, "dp", bit)
        after = yield None
        rows = block.shape[0]
        (block,), token = built([[(block, 0, rows), (got, 0, rows)]], after, fine)
        yield token
    half = block.shape[0] // 2
    beyond = trade(block, "dp", bits[-1])
    across = trade(block, "tensor", 1)
    after = yield None
    (low, high), token = built([[(across, 0, half)], [(beyond, half, half)]], after, fine)
    yield token
    far_low = trade(low, "dp", bits[-1])
    far_high = trade(high, "tensor", 1)
    after = yield None
    (mine, across), token = built(
        [[(block, 0, 2 * half), (beyond, 0, 2 * half)], [(across, 0, 2 * half), (far_low, 0, half), (far_high, 0, half)]],
        after, fine,
    )
    yield token
    yield Group([swap_cores(mine), swap_cores(across), mine, across], mine.shape[0], places, False)


def gather_flat(flat, parts):
    for bit in dp_bits(parts):
        flat = joined(flat, trade(flat, "dp", bit))
    flat = joined(flat, trade(flat, "tensor", 1))
    return joined(swap_cores(flat), flat).reshape(len(LINE), parts, -1)


def gather_common(shards, places, place_rows):
    parts = len(places)
    piece = shards[0].shape[0]
    model = parts * piece
    got = lax.all_gather(jnp.concatenate(shards, axis=1), ("tensor", "dp"), axis=0, tiled=True)
    groups, start = [], 0
    for shard in shards:
        width = shard.shape[1]
        if piece % 16:
            own = got[:, start : start + width].reshape(len(LINE), parts, piece, width)
            own = own[place_rows[0]][:, place_rows[1]].reshape(len(LINE), model, width)
            groups.append(Group([own[i] for i in range(len(LINE))], model, places, False))
        else:
            groups.append(Group([got], model, places, True))
            groups[-1].start = start
        start += width
    return groups


def added(left, right):
    return left.astype(F32) + right.astype(F32)


def merge_core_kernel(keep_ref, got_ref, across_ref, mine_a_ref, beyond_ref, mine_b_ref):
    total = added(keep_ref[...], got_ref[...]).astype(BF16)

    @pl.when(pl.program_id(0) == 0)
    def _():
        across_ref[...] = total[1]
        mine_a_ref[...] = total[0]

    @pl.when(pl.program_id(0) == 1)
    def _():
        beyond_ref[...] = total[:, 1]
        mine_b_ref[...] = total[:, 0]


def merge_core(keep, got, token):
    _, rows, width = keep.shape
    fourth = rows // 4
    view = (2, 2, 2, fourth, width)
    spec = pl.BlockSpec((2, 2, None, fourth, width), lambda t: (0, 0, t, 0, 0))
    return call(
        merge_core_kernel,
        "merge_core",
        2,
        [spec, spec],
        [whole((2, fourth, width))] * 4,
        [shaped((2, fourth, width), BF16)] * 4,
        [],
        keep.size,
        keep.size * 6,
        after=() if token is None else (token,),
        token=True,
    )(keep.reshape(view), got.reshape(view))


def merge_sides_kernel(a_ref, got_a_ref, b_ref, got_b_ref, keep_a_ref, send_a_ref, keep_b_ref, send_b_ref):
    keep_a_ref[...] = added(a_ref[0], got_a_ref[0]).astype(BF16)
    send_a_ref[...] = added(a_ref[1], got_a_ref[1]).astype(BF16)
    keep_b_ref[...] = added(b_ref[0], got_b_ref[0]).astype(BF16)
    send_b_ref[...] = added(b_ref[1], got_b_ref[1]).astype(BF16)


def merge_sides(a, got_a, b, got_b, token):
    _, rows, width = a.shape
    return call(
        merge_sides_kernel,
        "merge_sides",
        1,
        [whole((2, rows, width))] * 4,
        [whole((rows, width))] * 4,
        [shaped((rows, width), BF16)] * 4,
        [],
        a.size,
        a.size * 12,
        after=() if token is None else (token,),
        token=True,
    )(a, got_a, b, got_b)


def merge_pair_kernel(a_ref, got_a_ref, b_ref, got_b_ref, out_a_ref, out_b_ref):
    out_a_ref[...] = added(a_ref[...], got_a_ref[...]).astype(BF16)
    out_b_ref[...] = added(b_ref[...], got_b_ref[...]).astype(BF16)


def merge_pair(a, got_a, b, got_b, token):
    rows, width = a.shape
    return call(
        merge_pair_kernel,
        "merge_pair",
        1,
        [whole((rows, width))] * 4,
        [whole((rows, width))] * 2,
        [shaped((rows, width), BF16)] * 2,
        [],
        a.size,
        a.size * 12,
        after=() if token is None else (token,),
        token=True,
    )(a, got_a, b, got_b)


def merge_halves_kernel(a_ref, got_ref, keep_ref, send_ref):
    half = keep_ref.shape[0]
    keep_ref[...] = added(a_ref[:half], got_ref[:half]).astype(BF16)
    send_ref[...] = added(a_ref[half:], got_ref[half:]).astype(BF16)


def merge_halves(a, got, token):
    rows, width = a.shape
    return call(
        merge_halves_kernel,
        "merge_halves",
        1,
        [whole((rows, width))] * 2,
        [whole((rows // 2, width))] * 2,
        [shaped((rows // 2, width), BF16)] * 2,
        [],
        a.size,
        a.size * 6,
        after=() if token is None else (token,),
        token=True,
    )(a, got)


def scatter_group(send, keep, parts):
    bits = dp_bits(parts)
    got = swap_cores(send)
    token = yield None
    across, mine_a, beyond, mine_b, ran = merge_core(keep, got, token)
    got_a, got_b = trade(across, "tensor", 1), trade(beyond, "dp", bits[-1])
    token = yield ran
    keep_a, send_a, keep_b, send_b, ran = merge_sides(mine_a, got_a, mine_b, got_b, token)
    got_a, got_b = trade(send_a, "dp", bits[-1]), trade(send_b, "tensor", 1)
    token = yield ran
    keep, send, ran = merge_pair(keep_a, got_a, keep_b, got_b, token)
    for bit in reversed(bits[1:-1]):
        got = trade(send, "dp", bit)
        token = yield ran
        keep, send, ran = merge_halves(keep, got, token)
    got = trade(send, "dp", bits[0])
    token = yield ran
    yield added(keep, gated(got, token))


def on_device(
    tokens, cotangent, segment_ids, qkv_weight, out_weight, in_weight, down_weight,
    qv_bias, in_bias, row_bias, norm_gain, norm_shift,
):
    teams, parts = lax.axis_size("tensor"), lax.axis_size("dp")
    layers, _, piece, width = qkv_weight.shape
    heads = width // HD
    model = piece * parts
    units = in_weight.shape[2]
    tensor_at, dp_at = lax.axis_index("tensor"), lax.axis_index("dp")
    core = tensor_at % 2

    places = dp_places(parts)
    back = [places.index(i) for i in range(parts)]
    place_of = jnp.asarray(back)[jnp.arange(parts) ^ dp_at]
    line_of = jnp.asarray([LINE.index(i) for i in range(teams)])[jnp.arange(teams) ^ tensor_at]
    column = jnp.arange(model)
    source = (jnp.asarray(places)[column // piece] ^ dp_at) * piece + column % piece
    place = (column[:, None] == source[None, :]).astype(BF16)

    starts = (jnp.asarray(LINE) ^ tensor_at) * model
    rows = (jnp.asarray(places) ^ dp_at) * piece
    table = jnp.concatenate([starts, rows]).astype(jnp.int32)
    from_common = (jnp.asarray(LINE) ^ tensor_at, jnp.asarray(places) ^ dp_at)

    out_turned = jnp.swapaxes(out_weight, 1, 2)
    down_turned = jnp.swapaxes(down_weight, 1, 2)
    shards = []
    for layer in range(layers):
        shards.append(
            jnp.concatenate([qkv_weight[layer, i] for i in range(3)] + [out_turned[layer]], axis=1)
        )
        shards += [in_weight[layer], down_turned[layer]]

    weights = {}
    for layer in GATHERED:
        for kind, group in enumerate(gather_common(shards[3 * layer : 3 * layer + 3], places, from_common)):
            weights[3 * layer + kind] = group

    doc_ids = segment_ids[core, tensor_at // 2]
    current = dot_nn(to_sequence(tokens, core), place).astype(BF16)
    upstream = dot_nn(to_sequence(cotangent, core), place).astype(BF16)

    small = (qv_bias, in_bias, row_bias, norm_gain, norm_shift)
    lengths = [s.size for s in small]
    flat = gather_flat(jnp.concatenate([s.reshape(-1) for s in small]).reshape(1, -1), parts)
    edges = [0]
    for n in lengths:
        edges.append(edges[-1] + n)
    ordered = flat[:, place_of, : edges[2]]
    qv_all = (
        ordered[:, :, : edges[1]].reshape((teams, parts) + qv_bias.shape).transpose(2, 3, 0, 4, 1, 5)
        .reshape(layers, 2, teams, 1, width).astype(F32)
    )
    in_all = (
        ordered[:, :, edges[1] : edges[2]].reshape((teams, parts) + in_bias.shape).transpose(2, 0, 3, 1, 4)
        .reshape(layers, teams, 1, units).astype(F32)
    )
    vecs = (
        flat[0, :, edges[2] :].reshape((parts, 3) + row_bias.shape).transpose(2, 3, 1, 0, 4)
        .reshape(layers, 2, 3, model).astype(F32)
    )

    coming = {at: gather_group(shard, places) for at, shard in enumerate(shards) if at not in weights}
    for group in coming.values():
        next(group)
    steps = len(dp_bits(parts)) - 1
    last = ()

    def turn(index, after=()):
        nonlocal last
        last = (coming[index].send(tuple(last) + tuple(after)),)
        return next(coming[index])

    ready = (qv_all, in_all, vecs, current, upstream)
    saved = []
    for layer in range(layers):
        at = 3 * layer
        entered = current
        if at in coming:
            for _ in range(steps):
                turn(at)
            for _ in range(steps - 1):
                turn(at + 1)
            turn(at, ready)
            turn(at + 1)
            weights[at] = turn(at)
            for _ in range(steps - 1):
                turn(at + 2)
        qkv, prob, context, normal_one, scale_one, token = attend(
            table, entered, weights[at], qv_all[layer, 0], qv_all[layer, 1], vecs[layer, 0], doc_ids, last
        )
        last = (token,)
        if at in coming:
            turn(at + 1)
            turn(at + 2)
            weights[at + 1] = turn(at + 1)
            turn(at + 2)
            weights[at + 2] = turn(at + 2)
        low, active, slope, current, normal_two, scale_two, token = forward(
            table, normal_one, vecs[layer, 0], vecs[layer, 1], in_all[layer], weights[at + 1], weights[at + 2], last
        )
        last = (token,)
        saved.append(
            (entered, qkv, prob, context, normal_one, scale_one, low, active, slope, normal_two, scale_two)
        )
    smalls = [None] * layers
    owned, flights, ran, settled = {}, {}, [], ()
    fine = piece % 16 == 0

    def launch(key, grads):
        if key not in SCATTERED:
            flights[key] = scatter_group(*grads, parts)
            next(flights[key])
            return
        if not fine:
            grads = [
                joined(*grads).reshape(teams, parts, piece, -1)[line_of][:, place_of]
                .reshape(teams * model, -1)
            ]
        owned[key] = lax.psum_scatter(
            grads[0], ("tensor", "dp"), scatter_dimension=0, tiled=True
        ).astype(F32)

    def advance(keys, token):
        made = []
        for key in keys:
            got = flights[key].send(token)
            if got.shape != (8, 128):
                owned[key] = got
                del flights[key]
            else:
                made.append(got)
        return tuple(made)

    last = ()

    def push(*keys):
        nonlocal last
        for key in keys:
            if key in flights:
                last = advance([key], last[0] if last else None) or last

    for layer in reversed(range(layers)):
        (entered, qkv, prob, context, normal_one, scale_one, low, active, slope, normal_two, scale_two) = saved[layer]
        *grads, grad_one, sums_two, sums_one, unit_sums, token = forward_back(
            table, upstream, normal_two, scale_two, vecs[layer, 1], active, slope, weights[3 * layer + 1],
            weights[3 * layer + 2], low, normal_one, scale_one, vecs[layer, 0], (layer, 1) in SCATTERED and fine, last,
        )
        last = (token,)
        launch((layer, 1), grads)
        push(*flights)
        *grads, upstream, qkv_sums, token = attend_back(
            table, entered, grad_one, weights[3 * layer], qkv, prob, context, (layer, 0) in SCATTERED and fine, last,
        )
        last = (token,)
        launch((layer, 0), grads)
        smalls[layer] = (qkv_sums, unit_sums, sums_one, sums_two)
        push(*flights)
    keys = list(flights)
    token = last[0]
    for layer in range(layers):
        qkv_sums, unit_sums, sums_one, sums_two = (gated(s, token) for s in smalls[layer])
        row_sums = jnp.stack([sums_one, sums_two]).reshape(6, parts, piece)[:, place_of]
        smalls[layer] = (qkv_sums[line_of], unit_sums[line_of], row_sums)
    sizes = [s.size for s in smalls[0]]
    flat = jnp.concatenate([s.reshape(-1) for layer in smalls for s in layer]).reshape(-1, 128)
    rounds = [("tensor", bit) for bit in range(teams.bit_length() - 1)]
    rounds += [("dp", bit) for bit in range(parts.bit_length() - 1)]
    output = from_sequence(reorder(current, place, last), core)
    grad_tokens = from_sequence(reorder(upstream, place, last), core)
    while flights:
        for key in list(flights):
            got = trade(flat, *rounds.pop(0)) if rounds else None
            push(key)
            if got is not None:
                flat = flat + gated(got, last[0])
    for axis, bit in rounds:
        flat = flat + trade(flat, axis, bit)
    grads = [[owned[layer, 0], owned[layer, 1][:, :units], owned[layer, 1][:, units:]] for layer in range(layers)]

    flat = flat.reshape(layers, -1)
    qkv_sums = flat[:, : sizes[0]].reshape(layers, teams, 3, heads, parts, -1)
    qkv_sums = lax.dynamic_index_in_dim(qkv_sums, tensor_at, 1, keepdims=False)
    qkv_sums = lax.dynamic_index_in_dim(qkv_sums, dp_at, 3, keepdims=False)
    grad_qv = jnp.stack([qkv_sums[:, 0], qkv_sums[:, 2]], axis=1)
    unit_sums = flat[:, sizes[0] : sizes[0] + sizes[1]].reshape(layers, teams, units // HD, parts, -1)
    unit_sums = lax.dynamic_index_in_dim(unit_sums, tensor_at, 1, keepdims=False)
    grad_unit = lax.dynamic_index_in_dim(unit_sums, dp_at, 2, keepdims=False)
    row_sums = flat[:, sizes[0] + sizes[1] :].reshape(layers, 2, 3, parts, piece)
    row_sums = lax.dynamic_index_in_dim(row_sums, dp_at, 3, keepdims=False)

    grad_attn = jnp.stack([g[0] for g in grads])
    grad_qkv = jnp.stack(
        [grad_attn[:, :, i * width : (i + 1) * width] for i in range(3)], axis=1
    )
    return (
        output,
        grad_tokens,
        grad_qkv,
        jnp.swapaxes(grad_attn[:, :, 3 * width :], 1, 2),
        jnp.stack([g[1] for g in grads]),
        jnp.swapaxes(jnp.stack([g[2] for g in grads]), 1, 2),
        grad_qv,
        grad_unit,
        row_sums[:, :, 2],
        row_sums[:, :, 0],
        row_sums[:, :, 1],
    )


def solution(mesh):
    placed = (
        P(None, ("dp", "tensor"), None),
        P(None, ("dp", "tensor"), None),
        P(None, "dp", None),
        P(None, None, "dp", "tensor"),
        P(None, "tensor", "dp"),
        P(None, "dp", "tensor"),
        P(None, "tensor", "dp"),
        P(None, None, "tensor", "dp"),
        P(None, "tensor", "dp"),
        P(None, None, "dp"),
        P(None, None, "dp"),
        P(None, None, "dp"),
    )
    return jax.shard_map(
        on_device,
        mesh=mesh,
        in_specs=placed,
        out_specs=(
            P(None, ("dp", "tensor"), None),
            P(None, ("dp", "tensor"), None),
            P(None, None, "dp", "tensor"),
            P(None, "tensor", "dp"),
            P(None, "dp", "tensor"),
            P(None, "tensor", "dp"),
            P(None, None, "tensor", "dp"),
            P(None, "tensor", "dp"),
            P(None, None, "dp"),
            P(None, None, "dp"),
            P(None, None, "dp"),
        ),
        check_vma=False,
    )
```

```python
from functools import partial

import jax
import jax.numpy as jnp
from jax import lax
from jax.experimental import pallas as pl
from jax.experimental.pallas import tpu as pltpu
from jax.sharding import PartitionSpec as P

HD = 64
NORM_EPSILON = 1e-12
MASK_VALUE = -1000000000.0
F32 = jnp.float32
BF16 = jnp.bfloat16
STREAM_BYTES = 60 * 1024 * 1024
MERGE_BYTES = 32 * 1024 * 1024
FORWARD_SCALE, BACKWARD_SCALE = 0.25, 2000


def lasting(microseconds, scale):
    return pl.CostEstimate(flops=int(1.15e9 * microseconds * scale), bytes_accessed=0, transcendentals=0)


ROOT_HALF = 0.7071067811865476
ROOT_TWO_PI = 0.3989422804014327

LINE = (1, 3, 0, 2)

GATHERED = (1,)
SCATTERED = ()


def dot_nn(left, right):
    return lax.dot_general(left, right, (((1,), (0,)), ((), ())), preferred_element_type=F32)


def dot_nt(left, right):
    return lax.dot_general(left, right, (((1,), (1,)), ((), ())), preferred_element_type=F32)


def dot_tn(left, right):
    return lax.dot_general(left, right, (((0,), (0,)), ((), ())), preferred_element_type=F32)


def normed_rows(values):
    centre = values - jnp.mean(values, axis=-1, keepdims=True)
    spread = jnp.mean(centre * centre, axis=-1, keepdims=True)
    scale = lax.rsqrt(spread + NORM_EPSILON)
    return centre * scale, scale


def norm_back(upstream, normal, scale, gain):
    grad = upstream * gain
    mean_grad = jnp.mean(grad, axis=-1, keepdims=True)
    mean_both = jnp.mean(grad * normal, axis=-1, keepdims=True)
    return scale * (grad - mean_grad - normal * mean_both)


def token_sums(upstream, normal, result):
    return jnp.concatenate(
        [
            jnp.sum(upstream * normal, axis=0, keepdims=True),
            jnp.sum(upstream, axis=0, keepdims=True),
            jnp.sum(result, axis=0, keepdims=True),
        ],
        axis=0,
    )


def turned(values):
    return values.astype(F32).T.astype(BF16)


ANYWHERE = pl.BlockSpec(memory_space=pl.ANY)
IN_VMEM = pl.BlockSpec(memory_space=pltpu.VMEM)
IN_SMEM = pl.BlockSpec(memory_space=pltpu.SMEM)


def shaped(shape, dtype):
    return jax.ShapeDtypeStruct(tuple(shape), dtype)


class Rows:
    def __init__(self, array, split=False):
        self.operands = [array]
        self.scratch = [
            pltpu.VMEM(array.shape, array.dtype),
            pltpu.SemaphoreType.DMA((array.shape[0] if split else 1,)),
        ]

    def bind(self, refs, scratch, table):
        (self.ref,), (self.held, self.sems) = refs, scratch
        return self

    def copy(self, index):
        if index is None:
            return pltpu.make_async_copy(self.ref, self.held, self.sems.at[0])
        return pltpu.make_async_copy(self.ref.at[index], self.held.at[index], self.sems.at[index])

    def start(self, index=None):
        self.copy(index).start()

    def wait(self, index=None):
        self.copy(index).wait()


class Weights:
    def __init__(self, group, start, width):
        self.group, self.cols = group, pl.ds(group.start + start, width)
        self.operands = list(group.arrays)
        model = group.model
        self.scratch = [
            pltpu.VMEM((len(LINE), model, width), BF16),
            pltpu.SemaphoreType.DMA((len(LINE), len(group.places))),
        ]

    def bind(self, refs, scratch, table):
        self.refs, (self.held, self.sems), self.table = refs, scratch, table
        return self

    def copies(self, index):
        if not self.group.common and self.group.pitch * len(self.group.places) == self.group.model:
            yield pltpu.make_async_copy(
                self.refs[index].at[:, self.cols], self.held.at[index], self.sems.at[index, 0]
            )
            return
        places = len(self.group.places)
        piece = self.group.model // places
        for place in range(places):
            if self.group.common:
                ref = self.refs[0]
                row = pl.multiple_of(self.table[index] + self.table[len(LINE) + place], piece)
            else:
                ref, row = self.refs[index], place * self.group.pitch
            yield pltpu.make_async_copy(
                ref.at[pl.ds(row, piece), self.cols],
                self.held.at[index, pl.ds(place * piece, piece)],
                self.sems.at[index, place],
            )

    def start(self, index):
        for copy in self.copies(index):
            copy.start()

    def wait(self, index):
        for copy in self.copies(index):
            copy.wait()


class Result:
    def __init__(self, shape, dtype, split=False):
        self.shapes = [shaped(shape, dtype)]
        self.indices = range(shape[0]) if split else (None,)
        self.scratch = [
            pltpu.VMEM(shape, dtype),
            pltpu.SemaphoreType.DMA((shape[0] if split else 1,)),
        ]

    def bind(self, refs, scratch, table):
        (self.ref,), (self.held, self.sems) = refs, scratch
        return self

    def copy(self, index):
        if index is None:
            return pltpu.make_async_copy(self.held, self.ref, self.sems.at[0])
        return pltpu.make_async_copy(self.held.at[index], self.ref.at[index], self.sems.at[index])

    def start(self, index=None):
        self.copy(index).start()

    def finish(self):
        for index in self.indices:
            self.copy(index).wait()


class Grads:
    def __init__(self, model, width, places, common):
        self.model, self.places, self.common = model, places, common
        teams = len(LINE)
        if common:
            self.shapes = [shaped((teams * model, width), BF16)]
        else:
            self.shapes = [shaped((2, model, width), BF16)] * 2
        self.scratch = [
            pltpu.VMEM((teams, model, width), BF16),
            pltpu.SemaphoreType.DMA((teams, len(places) if common else 1)),
        ]

    def bind(self, refs, scratch, table):
        self.refs, (self.held, self.sems), self.table = refs, scratch, table
        return self

    def copies(self, index):
        if not self.common:
            yield pltpu.make_async_copy(
                self.held.at[index], self.refs[index // 2].at[index % 2], self.sems.at[index, 0]
            )
            return
        places = len(self.places)
        piece = self.model // places
        for place in range(places):
            row = pl.multiple_of(self.table[index] + self.table[len(LINE) + place], piece)
            yield pltpu.make_async_copy(
                self.held.at[index, pl.ds(place * piece, piece)],
                self.refs[0].at[pl.ds(row, piece)],
                self.sems.at[index, place],
            )

    def start(self, index):
        for copy in self.copies(index):
            copy.start()

    def finish(self):
        for index in range(len(LINE)):
            for copy in self.copies(index):
                copy.wait()


def streamed(body, name, table, ins, outs, scratch=(), after=(), lasts=15, scale=FORWARD_SCALE):
    waits = len(after)
    operands = [array for item in ins for array in item.operands]
    shapes = [shape for item in outs for shape in item.shapes]

    def wrapped(*refs):
        refs = list(refs)

        def take(count):
            taken = refs[:count]
            del refs[:count]
            return taken

        (table_ref,) = take(1)
        in_refs = [take(len(item.operands)) for item in ins]
        take(waits)
        out_refs = [take(len(item.shapes)) for item in outs]
        (token_ref,) = take(1)
        token_ref[...] = jnp.zeros((8, 128), F32)
        inlets = [item.bind(own, take(len(item.scratch)), table_ref) for item, own in zip(ins, in_refs)]
        outlets = [item.bind(own, take(len(item.scratch)), table_ref) for item, own in zip(outs, out_refs)]
        body(inlets, outlets, *refs)
        for outlet in outlets:
            outlet.finish()

    kernel = pl.pallas_call(
        wrapped,
        in_specs=[IN_SMEM] + [ANYWHERE] * (len(operands) + waits),
        out_specs=[ANYWHERE] * len(shapes) + [IN_VMEM],
        out_shape=shapes + [shaped((8, 128), F32)],
        scratch_shapes=[entry for item in list(ins) + list(outs) for entry in item.scratch] + list(scratch),
        compiler_params=pltpu.CompilerParams(vmem_limit_bytes=STREAM_BYTES),
        cost_estimate=lasting(lasts, scale),
        name=name,
    )
    return kernel(table, *operands, *after)


def attend_body(inlets, outlets, low_ref):
    x, doc_col, doc_row, vec, q_bias, v_bias, weights = inlets
    qkv, prob, context, normal_out, scale_out = outlets
    steps, _, width = q_bias.held.shape
    heads = width // HD
    for inlet in (doc_col, doc_row, vec, q_bias, v_bias, x):
        inlet.start()
    weights.start(0)
    weights.start(1)
    for inlet in (doc_col, doc_row, vec, q_bias, v_bias, x):
        inlet.wait()
    low_ref[...] = x.held[...].astype(BF16)
    total = x.held[...].astype(F32) + vec.held[0:1]
    same_doc = doc_col.held[...] == doc_row.held[...]
    for step in range(steps):
        weights.wait(step)
        if step + 2 < steps:
            weights.start(step + 2)
        projected = dot_nn(low_ref[...], weights.held[step, :, : 3 * width])
        queries = (projected[:, :width] + q_bias.held[step]).astype(BF16) * jnp.asarray(0.125, BF16)
        key_rows = projected[:, width : 2 * width].astype(BF16)
        value_full = projected[:, 2 * width :] + v_bias.held[step]
        qkv.held[step, :, :width] = queries
        qkv.held[step, :, width : 2 * width] = key_rows
        qkv.held[step, :, 2 * width :] = value_full.astype(BF16)
        qkv.start(step)
        value_turned = turned(value_full)
        parts = []
        for head in range(heads):
            cols = slice(head * HD, (head + 1) * HD)
            scores = jnp.where(same_doc, dot_nt(key_rows[:, cols], queries[:, cols]), MASK_VALUE)
            expo = jnp.exp(scores - jnp.max(scores, axis=0, keepdims=True))
            chances = (expo * (1.0 / jnp.sum(expo, axis=0, keepdims=True))).astype(BF16)
            prob.held[step * heads + head] = chances
            prob.start(step * heads + head)
            parts.append(dot_nn(value_turned[cols], chances))
        context_turned = jnp.concatenate(parts, axis=0)
        context.held[step] = context_turned.astype(BF16)
        context.start(step)
        total = total + dot_nt(context_turned.T.astype(BF16), weights.held[step, :, 3 * width :])
    normal, scale = normed_rows(total)
    normal_out.held[...] = normal
    scale_out.held[...] = scale
    normal_out.start()
    scale_out.start()


def attend(table, x, weights, q_bias, v_bias, vec, doc_ids, after=()):
    steps, width = q_bias.shape[0], q_bias.shape[2]
    rows, model = x.shape
    heads = width // HD
    return streamed(
        attend_body,
        "attend",
        table,
        [
            Rows(x), Rows(doc_ids.reshape(rows, 1)), Rows(doc_ids.reshape(1, rows)), Rows(vec), Rows(q_bias),
            Rows(v_bias), Weights(weights, 0, 4 * width),
        ],
        [
            Result((steps, rows, 3 * width), BF16, True),
            Result((steps * heads, rows, rows), BF16, True),
            Result((steps, width, rows), BF16, True),
            Result((rows, model), F32),
            Result((rows, 1), F32),
        ],
        [pltpu.VMEM((rows, model), BF16)],
        after=after,
    )


def forward_body(inlets, outlets, low_ref):
    normal, vec, vec_two, bias, first, second = inlets
    low_out, active, slope, out, normal_two, scale_two = outlets
    steps = bias.held.shape[0]
    for inlet in (vec, vec_two, bias, normal):
        inlet.start()
    for step in range(2):
        first.start(step)
        second.start(step)
    for inlet in (vec, vec_two, bias, normal):
        inlet.wait()
    rows = normal.held[...] * vec.held[1:2] + vec.held[2:3]
    low_ref[...] = rows.astype(BF16)
    low_out.held[...] = rows.astype(BF16)
    low_out.start()
    total = rows + vec_two.held[0:1]
    for step in range(steps):
        first.wait(step)
        second.wait(step)
        if step + 2 < steps:
            first.start(step + 2)
            second.start(step + 2)
        hidden = dot_nn(low_ref[...], first.held[step]) + bias.held[step]
        below = 0.5 + 0.5 * lax.erf(hidden * ROOT_HALF)
        value = (hidden * below).astype(BF16)
        active.held[step] = value
        slope.held[step] = (below + hidden * (jnp.exp(hidden * hidden * -0.5) * ROOT_TWO_PI)).astype(BF16)
        active.start(step)
        slope.start(step)
        total = total + dot_nt(value, second.held[step])
    normal_value, scale = normed_rows(total)
    normal_two.held[...] = normal_value
    scale_two.held[...] = scale
    out.held[...] = normal_value * vec_two.held[1:2] + vec_two.held[2:3]
    for outlet in (normal_two, scale_two, out):
        outlet.start()


def forward(table, normal, vec, vec_two, bias, first, second, after=()):
    steps, _, width = bias.shape
    rows, model = normal.shape
    return streamed(
        forward_body,
        "forward",
        table,
        [
            Rows(normal), Rows(vec), Rows(vec_two), Rows(bias),
            Weights(first, 0, width), Weights(second, 0, width),
        ],
        [
            Result((rows, model), BF16),
            Result((steps, rows, width), BF16, True),
            Result((steps, rows, width), BF16, True),
            Result((rows, model), F32),
            Result((rows, model), F32),
            Result((rows, 1), F32),
        ],
        [pltpu.VMEM((rows, model), BF16)],
        after=after,
    )


def forward_back_body(inlets, outlets, low_two_ref):
    up, normal_two, scale_two, vec_two, active, slope, second, first, low, normal, scale, vec = inlets
    grads, grad_one, sums_two, sums_one, unit_sums = outlets
    steps, _, width = active.held.shape
    for inlet in (scale_two, vec_two, up, normal_two):
        inlet.start()
    for inlet in (scale_two, vec_two, up, normal_two):
        inlet.wait()

    def bring(step):
        for inlet in (active, second, slope, first):
            inlet.start(step)

    bring(0)
    low.start()
    bring(1)
    upstream, normal_value = up.held[...].astype(F32), normal_two.held[...]
    grad = norm_back(upstream, normal_value, scale_two.held[...], vec_two.held[1:2])
    low_two_ref[...] = grad.astype(BF16)
    total = grad
    sums_two.held[...] = token_sums(upstream, normal_value, grad)
    sums_two.start()
    for step in range(steps):
        for inlet in (active, second, slope, first):
            inlet.wait(step)
        if step == 0:
            low.wait()
        if step + 2 < steps:
            bring(step + 2)
        elif step + 2 == steps:
            for inlet in (scale, vec, normal):
                inlet.start()
        grads.held[step, :, width:] = dot_tn(low_two_ref[...], active.held[step]).astype(BF16)
        value = (dot_nn(low_two_ref[...], second.held[step]) * slope.held[step].astype(F32)).astype(BF16)
        unit_sums.held[step] = jnp.sum(value.astype(F32), axis=0, keepdims=True)
        grads.held[step, :, :width] = dot_tn(low.held[...], value).astype(BF16)
        grads.start(step)
        unit_sums.start(step)
        total = total + dot_nt(value, first.held[step])
    for inlet in (scale, vec, normal):
        inlet.wait()
    normal_value = normal.held[...]
    grad = norm_back(total, normal_value, scale.held[...], vec.held[1:2])
    grad_one.held[...] = grad
    sums_one.held[...] = token_sums(total, normal_value, grad)
    grad_one.start()
    sums_one.start()


def forward_back(
    table, upstream, normal_two, scale_two, vec_two, active, slope, first, second, low, normal, scale, vec, common,
    after=(),
):
    steps, rows, width = active.shape
    model = low.shape[1]
    return streamed(
        forward_back_body,
        "forward_back",
        table,
        [
            Rows(upstream), Rows(normal_two), Rows(scale_two), Rows(vec_two), Rows(active, True), Rows(slope, True),
            Weights(second, 0, width), Weights(first, 0, width), Rows(low), Rows(normal), Rows(scale), Rows(vec),
        ],
        [
            Grads(model, 2 * width, first.places, common),
            Result((rows, model), F32),
            Result((3, model), F32),
            Result((3, model), F32),
            Result((steps, 1, width), F32, True),
        ],
        [pltpu.VMEM((rows, model), BF16)],
        after=after,
        lasts=19,
        scale=BACKWARD_SCALE,
    )


def attend_back_body(inlets, outlets, low_ref, x_low_ref):
    x, grad_one, qkv, prob, context, weights, unit_sums, sums_one, sums_two = inlets
    grads, grad_x = outlets
    places = len(grads.places)
    model = x.held.shape[1]
    piece, pitch = model // places, grads.held.shape[1] // places
    steps, width, _ = context.held.shape
    heads = prob.held.shape[0] // steps

    def bring(step):
        weights.start(step)
        qkv.start(step)
        for head in range(heads):
            prob.start(step * heads + head)
        context.start(step)

    grad_one.start()
    bring(0)
    x.start()
    bring(1)
    for inlet in (unit_sums, sums_one, sums_two):
        inlet.start()
    grad_one.wait()
    low_ref[...] = grad_one.held[...].astype(BF16)
    total = grad_one.held[...]
    for inlet in (unit_sums, sums_one, sums_two):
        inlet.wait()
    sums = jnp.concatenate([sums_one.held[...], sums_two.held[...]], axis=0)
    for step in range(steps):
        weights.wait(step)
        qkv.wait(step)
        context.wait(step)
        for head in range(heads):
            prob.wait(step * heads + head)
        if step == 0:
            x.wait()
            x_low_ref[...] = x.held[...].astype(BF16)
        if step + 2 < steps:
            bring(step + 2)
        block = qkv.held[step]
        queries, key_rows = block[:, :width], block[:, width : 2 * width]
        value_rows = block[:, 2 * width :]
        key_turned = turned(key_rows)
        grad_context = dot_nn(low_ref[...], weights.held[step, :, 3 * width :]).astype(BF16)
        grad_q, grad_k, grad_v = [], [], []
        for head in range(heads):
            cols = slice(head * HD, (head + 1) * HD)
            low_weights = prob.held[step * heads + head]
            chances = low_weights.astype(F32)
            part = chances * dot_nt(value_rows[:, cols], grad_context[:, cols])
            centre = jnp.sum(part, axis=0, keepdims=True)
            grad_scores = (part - chances * centre).astype(BF16)
            grad_v.append(dot_nn(low_weights, grad_context[:, cols]))
            grad_k.append(dot_nn(grad_scores, queries[:, cols]))
            grad_q.append(dot_nn(key_turned[cols], grad_scores))
        stacked = jnp.concatenate(
            [(jnp.concatenate(grad_q, axis=0) * 0.125).T] + grad_k + grad_v, axis=1
        ).astype(BF16)
        qkv_grad = dot_tn(x_low_ref[...], stacked)
        out_grad = dot_tn(low_ref[...], turned(context.held[step]))
        qkv_sums = jnp.sum(stacked.astype(F32), axis=0, keepdims=True)
        top = jnp.concatenate(
            [jnp.concatenate([qkv_sums, jnp.zeros((1, width), F32)], axis=1), unit_sums.held[step]], axis=0
        )
        for place in range(places):
            rows = slice(place * piece, (place + 1) * piece)
            at = place * pitch
            grads.held[step, at : at + piece, : 3 * width] = qkv_grad[rows].astype(BF16)
            grads.held[step, at : at + piece, 3 * width :] = out_grad[rows].astype(BF16)
            own = jnp.concatenate([sums[:, rows], jnp.zeros((6, 4 * width - piece), F32)], axis=1)
            grads.held[step, at + pitch - EXTRA : at + pitch] = jnp.concatenate(
                [top, own, jnp.zeros((EXTRA - 8, 4 * width), F32)], axis=0
            ).astype(BF16)
        grads.start(step)
        total = total + dot_nt(stacked, weights.held[step, :, : 3 * width])
    grad_x.held[...] = total
    grad_x.start()


def attend_back(
    table, x, grad_one, weights, qkv, prob, context, unit_sums, sums_one, sums_two, after=()
):
    steps, width, rows = context.shape
    model = x.shape[1]
    return streamed(
        attend_back_body,
        "attend_back",
        table,
        [
            Rows(x), Rows(grad_one), Rows(qkv, True), Rows(prob, True), Rows(context, True),
            Weights(weights, 0, 4 * width), Rows(unit_sums), Rows(sums_one), Rows(sums_two),
        ],
        [
            Grads(len(weights.places) * (-(-model // len(weights.places) // 16) * 16 + EXTRA), 4 * width, weights.places, False),
            Result((rows, model), F32),
        ],
        [pltpu.VMEM((rows, model), BF16), pltpu.VMEM((rows, model), BF16)],
        after=after,
        lasts=22,
        scale=BACKWARD_SCALE,
    )


def whole(shape):
    return pl.BlockSpec(shape, lambda t: (0,) * len(shape))


def call(body, name, steps, in_specs, out_specs, out_shape, scratch, flops, moved, after=(), token=False):
    single = not isinstance(out_shape, list)
    out_specs = [out_specs] if single else list(out_specs)
    out_shape = [out_shape] if single else list(out_shape)
    inputs, outputs, waits = len(in_specs), len(out_shape), len(after)
    if token:
        out_specs.append(whole((8, 128)))
        out_shape.append(shaped((8, 128), F32))

    def wrapped(*refs):
        made = refs[inputs + waits :]
        if token:
            made[outputs][...] = jnp.zeros((8, 128), F32)
        body(*refs[:inputs], *made[:outputs], *made[outputs + token :])

    kernel = pl.pallas_call(
        wrapped,
        grid=(steps,),
        in_specs=list(in_specs) + [ANYWHERE] * waits,
        out_specs=out_specs,
        out_shape=out_shape,
        scratch_shapes=scratch,
        compiler_params=pltpu.CompilerParams(
            dimension_semantics=("arbitrary",), vmem_limit_bytes=MERGE_BYTES
        ),
        cost_estimate=lasting(2, BACKWARD_SCALE),
        name=name,
    )

    def run(*args):
        made = kernel(*args, *after)
        if not single or token:
            return made
        return made[0]

    return run


def reorder_kernel(values_ref, place_ref, out_ref):
    values = values_ref[...]
    high = values.astype(BF16)
    low = (values - high.astype(F32)).astype(BF16)
    place = place_ref[...]
    out_ref[...] = dot_nt(high, place) + dot_nt(low, place)


def reorder(values, place, after=()):
    rows, model = values.shape
    return call(
        reorder_kernel,
        "reorder",
        1,
        [whole((rows, model)), whole((model, model))],
        whole((rows, model)),
        shaped((rows, model), F32),
        [],
        4 * rows * model * model,
        8 * rows * model,
        after=after,
    )(values, place)


def dp_bits(parts):
    return list(range(1, parts.bit_length() - 1))[::-1] + [0]


def dp_places(parts):
    bits = dp_bits(parts)
    return [sum(((place >> k) & 1) << bit for k, bit in enumerate(bits)) for place in range(parts)]


def trade(values, axis, bit):
    return lax.ppermute(values, axis, [(i, i ^ (1 << bit)) for i in range(lax.axis_size(axis))])


def swap_cores(values):
    return trade(values, "tensor", 0)


def to_sequence(blocks, core):
    mine = lax.dynamic_index_in_dim(blocks, core, 0, keepdims=False)
    other = lax.dynamic_index_in_dim(blocks, 1 - core, 0, keepdims=False)
    got = swap_cores(other)
    return jnp.concatenate(
        [jnp.where(core == 0, mine, got), jnp.where(core == 0, got, mine)], axis=0
    )


def from_sequence(values, core):
    half = values.shape[0] // 2
    mine = lax.dynamic_slice_in_dim(values, core * half, half, 0)
    got = swap_cores(lax.dynamic_slice_in_dim(values, (1 - core) * half, half, 0))
    return jnp.stack([jnp.where(core == 0, mine, got), jnp.where(core == 0, got, mine)])


def joined(*blocks):
    return jnp.concatenate(blocks, axis=0)


def gated(values, token):
    return values if token is None else values + token[0, 0].astype(values.dtype)


class Group:
    def __init__(self, arrays, model, places, common):
        self.arrays, self.model, self.places, self.common = arrays, model, places, common
        self.start, self.pitch = 0, model // len(places)


def mark(*arrays):
    def body(*refs):
        refs[-1][...] = jnp.zeros((8, 128), F32)

    return pl.pallas_call(
        body,
        in_specs=[ANYWHERE] * len(arrays),
        out_specs=IN_VMEM,
        out_shape=shaped((8, 128), F32),
        cost_estimate=lasting(0.5, FORWARD_SCALE),
        name="mark",
    )(*arrays)


def moved(plan, after):
    arrays = []
    for parts in plan:
        for array, _, _ in parts:
            if not any(array is other for other in arrays):
                arrays.append(array)
    steps = []
    for out, parts in enumerate(plan):
        at = 0
        for array, start, rows in parts:
            source = [array is other for other in arrays].index(True)
            steps.append((source, start, out, at, rows))
            at += rows
    shapes = [
        shaped((sum(rows for _, _, rows in parts),) + parts[0][0].shape[1:], parts[0][0].dtype) for parts in plan
    ]
    count, waits = len(arrays), len(after)

    def body(*refs):
        refs = list(refs)
        sources, results = refs[:count], refs[count + waits : count + waits + len(plan)]
        token_ref, *held = refs[count + waits + len(plan) : -2]
        sems, out_sems = refs[-2:]
        token_ref[...] = jnp.zeros((8, 128), F32)
        brought = [
            pltpu.make_async_copy(
                sources[source].at[pl.ds(start, rows)], held[out].at[pl.ds(at, rows)], sems.at[k]
            )
            for k, (source, start, out, at, rows) in enumerate(steps)
        ]
        for copy in brought:
            copy.start()
        for copy in brought:
            copy.wait()
        given = [pltpu.make_async_copy(held[k], results[k], out_sems.at[k]) for k in range(len(plan))]
        for copy in given:
            copy.start()
        for copy in given:
            copy.wait()

    return pl.pallas_call(
        body,
        in_specs=[ANYWHERE] * (count + waits),
        out_specs=[ANYWHERE] * len(shapes) + [IN_VMEM],
        out_shape=shapes + [shaped((8, 128), F32)],
        scratch_shapes=[pltpu.VMEM(shape.shape, shape.dtype) for shape in shapes]
        + [pltpu.SemaphoreType.DMA((len(steps),)), pltpu.SemaphoreType.DMA((len(plan),))],
        compiler_params=pltpu.CompilerParams(vmem_limit_bytes=MERGE_BYTES),
        cost_estimate=lasting(2, FORWARD_SCALE),
        name="moved",
    )(*arrays, *after)


def built(plan, after, fine):
    if fine:
        *made, token = moved(plan, after)
        return made, token
    token = mark(*after) if after else None
    made = [joined(*[gated(array[start : start + rows], token) for array, start, rows in parts]) for parts in plan]
    return made, mark(*made)


def gather_group(shard, places):
    parts = len(places)
    bits = dp_bits(parts)
    fine = shard.shape[0] % 16 == 0
    block = shard
    for bit in bits[:-1]:
        got = trade(block, "dp", bit)
        after = yield None
        rows = block.shape[0]
        (block,), token = built([[(block, 0, rows), (got, 0, rows)]], after, fine)
        yield token
    half = block.shape[0] // 2
    beyond = trade(block, "dp", bits[-1])
    across = trade(block, "tensor", 1)
    after = yield None
    (low, high), token = built([[(across, 0, half)], [(beyond, half, half)]], after, fine)
    yield token
    far_low = trade(low, "dp", bits[-1])
    far_high = trade(high, "tensor", 1)
    after = yield None
    (mine, across), token = built(
        [[(block, 0, 2 * half), (beyond, 0, 2 * half)], [(across, 0, 2 * half), (far_low, 0, half), (far_high, 0, half)]],
        after, fine,
    )
    yield token
    yield Group([swap_cores(mine), swap_cores(across), mine, across], mine.shape[0], places, False)


EXTRA = 16


def padded(rows, to):
    return jnp.pad(rows, ((0, to - rows.shape[0]), (0, 0)))


def without_extra(group, piece):
    parts = len(group.places)
    pitch = group.model // parts
    blocks = [array.reshape(parts, pitch, -1) for array in group.arrays]
    extra = jnp.stack([block[:, pitch - EXTRA :] for block in blocks])
    group.model = parts * piece
    if piece % 16:
        group.arrays = [block[:, :piece].reshape(parts * piece, -1) for block in blocks]
        pitch = piece
    group.pitch = pitch
    return group, extra


def gather_common(shards, places, place_rows):
    parts = len(places)
    piece = shards[0].shape[0]
    model = parts * piece
    got = lax.all_gather(jnp.concatenate(shards, axis=1), ("tensor", "dp"), axis=0, tiled=True)
    groups, start = [], 0
    for shard in shards:
        width = shard.shape[1]
        if piece % 16:
            own = got[:, start : start + width].reshape(len(LINE), parts, piece, width)
            own = own[place_rows[0]][:, place_rows[1]].reshape(len(LINE), model, width)
            groups.append(Group([own[i] for i in range(len(LINE))], model, places, False))
        else:
            groups.append(Group([got], model, places, True))
            groups[-1].start = start
        start += width
    return groups


def added(left, right):
    return left.astype(F32) + right.astype(F32)


def merge_core_kernel(keep_ref, got_ref, across_ref, mine_a_ref, beyond_ref, mine_b_ref):
    total = added(keep_ref[...], got_ref[...]).astype(BF16)

    @pl.when(pl.program_id(0) == 0)
    def _():
        across_ref[...] = total[1]
        mine_a_ref[...] = total[0]

    @pl.when(pl.program_id(0) == 1)
    def _():
        beyond_ref[...] = total[:, 1]
        mine_b_ref[...] = total[:, 0]


def merge_core(keep, got, token):
    _, rows, width = keep.shape
    fourth = rows // 4
    view = (2, 2, 2, fourth, width)
    spec = pl.BlockSpec((2, 2, None, fourth, width), lambda t: (0, 0, t, 0, 0))
    return call(
        merge_core_kernel,
        "merge_core",
        2,
        [spec, spec],
        [whole((2, fourth, width))] * 4,
        [shaped((2, fourth, width), BF16)] * 4,
        [],
        keep.size,
        keep.size * 6,
        after=() if token is None else (token,),
        token=True,
    )(keep.reshape(view), got.reshape(view))


def merge_sides_kernel(a_ref, got_a_ref, b_ref, got_b_ref, keep_a_ref, send_a_ref, keep_b_ref, send_b_ref):
    keep_a_ref[...] = added(a_ref[0], got_a_ref[0]).astype(BF16)
    send_a_ref[...] = added(a_ref[1], got_a_ref[1]).astype(BF16)
    keep_b_ref[...] = added(b_ref[0], got_b_ref[0]).astype(BF16)
    send_b_ref[...] = added(b_ref[1], got_b_ref[1]).astype(BF16)


def merge_sides(a, got_a, b, got_b, token):
    _, rows, width = a.shape
    return call(
        merge_sides_kernel,
        "merge_sides",
        1,
        [whole((2, rows, width))] * 4,
        [whole((rows, width))] * 4,
        [shaped((rows, width), BF16)] * 4,
        [],
        a.size,
        a.size * 12,
        after=() if token is None else (token,),
        token=True,
    )(a, got_a, b, got_b)


def merge_pair_kernel(a_ref, got_a_ref, b_ref, got_b_ref, out_a_ref, out_b_ref):
    out_a_ref[...] = added(a_ref[...], got_a_ref[...]).astype(BF16)
    out_b_ref[...] = added(b_ref[...], got_b_ref[...]).astype(BF16)


def merge_pair(a, got_a, b, got_b, token):
    rows, width = a.shape
    return call(
        merge_pair_kernel,
        "merge_pair",
        1,
        [whole((rows, width))] * 4,
        [whole((rows, width))] * 2,
        [shaped((rows, width), BF16)] * 2,
        [],
        a.size,
        a.size * 12,
        after=() if token is None else (token,),
        token=True,
    )(a, got_a, b, got_b)


def merge_halves_kernel(a_ref, got_ref, keep_ref, send_ref):
    half = keep_ref.shape[0]
    keep_ref[...] = added(a_ref[:half], got_ref[:half]).astype(BF16)
    send_ref[...] = added(a_ref[half:], got_ref[half:]).astype(BF16)


def merge_halves(a, got, token):
    rows, width = a.shape
    return call(
        merge_halves_kernel,
        "merge_halves",
        1,
        [whole((rows, width))] * 2,
        [whole((rows // 2, width))] * 2,
        [shaped((rows // 2, width), BF16)] * 2,
        [],
        a.size,
        a.size * 6,
        after=() if token is None else (token,),
        token=True,
    )(a, got)


def scatter_group(send, keep, parts):
    bits = dp_bits(parts)
    got = swap_cores(send)
    token = yield None
    across, mine_a, beyond, mine_b, ran = merge_core(keep, got, token)
    got_a, got_b = trade(across, "tensor", 1), trade(beyond, "dp", bits[-1])
    token = yield ran
    keep_a, send_a, keep_b, send_b, ran = merge_sides(mine_a, got_a, mine_b, got_b, token)
    got_a, got_b = trade(send_a, "dp", bits[-1]), trade(send_b, "tensor", 1)
    token = yield ran
    keep, send, ran = merge_pair(keep_a, got_a, keep_b, got_b, token)
    for bit in reversed(bits[1:-1]):
        got = trade(send, "dp", bit)
        token = yield ran
        keep, send, ran = merge_halves(keep, got, token)
    got = trade(send, "dp", bits[0])
    token = yield ran
    yield added(keep, gated(got, token))


def on_device(
    tokens, cotangent, segment_ids, qkv_weight, out_weight, in_weight, down_weight,
    qv_bias, in_bias, row_bias, norm_gain, norm_shift,
):
    teams, parts = lax.axis_size("tensor"), lax.axis_size("dp")
    layers, _, piece, width = qkv_weight.shape
    heads = width // HD
    model = piece * parts
    units = in_weight.shape[2]
    tensor_at, dp_at = lax.axis_index("tensor"), lax.axis_index("dp")
    core = tensor_at % 2

    places = dp_places(parts)
    column = jnp.arange(model)
    source = (jnp.asarray(places)[column // piece] ^ dp_at) * piece + column % piece
    place = (column[:, None] == source[None, :]).astype(BF16)

    starts = (jnp.asarray(LINE) ^ tensor_at) * model
    rows = (jnp.asarray(places) ^ dp_at) * piece
    table = jnp.concatenate([starts, rows]).astype(jnp.int32)
    from_common = (jnp.asarray(LINE) ^ tensor_at, jnp.asarray(places) ^ dp_at)

    out_turned = jnp.swapaxes(out_weight, 1, 2)
    down_turned = jnp.swapaxes(down_weight, 1, 2)
    shards = []
    for layer in range(layers):
        shards.append(
            jnp.concatenate([qkv_weight[layer, i] for i in range(3)] + [out_turned[layer]], axis=1)
        )
        shards += [in_weight[layer], down_turned[layer]]

    weights = {}
    for layer in GATHERED:
        for kind, group in enumerate(gather_common(shards[3 * layer : 3 * layer + 3], places, from_common)):
            weights[3 * layer + kind] = group

    doc_ids = segment_ids[core, tensor_at // 2]
    current = dot_nn(to_sequence(tokens, core), place).astype(BF16)
    upstream = dot_nn(to_sequence(cotangent, core), place).astype(BF16)

    per = HD // parts
    lanes = [qv_bias[layer, i].reshape(-1) for layer in range(layers) for i in range(2)]
    lanes += [in_bias[layer].reshape(-1) for layer in range(layers)]
    lanes = jnp.concatenate(lanes)
    wide = shards[0].shape[1]
    vectors = jnp.stack([row_bias, norm_gain, norm_shift], axis=2).reshape(-1, piece)
    extra = jnp.concatenate(
        [jnp.pad(lanes, (0, wide - lanes.size))[None], jnp.pad(vectors, ((0, 0), (0, wide - piece)))]
    )
    filled = -(-piece // 16) * 16
    shards[0] = joined(padded(shards[0], filled), padded(extra, EXTRA))

    coming = {at: gather_group(shard, places) for at, shard in enumerate(shards) if at not in weights}
    for group in coming.values():
        next(group)
    steps = len(dp_bits(parts)) - 1
    last = ()

    def turn(index, after=()):
        nonlocal last
        last = (coming[index].send(tuple(last) + tuple(after)),)
        return next(coming[index])

    ready = (current, upstream)
    saved = []
    for layer in range(layers):
        at = 3 * layer
        entered = current
        if at in coming:
            for _ in range(steps):
                turn(at)
            for _ in range(steps - 1):
                turn(at + 1)
            turn(at, ready)
            turn(at + 1)
            weights[at] = turn(at)
            if at == 0:
                weights[0], extra = without_extra(weights[0], piece)
                vecs = (
                    extra[0, :, 1 : 1 + 6 * layers, :piece].transpose(1, 0, 2)
                    .reshape(layers, 2, 3, model).astype(F32)
                )
                widths = [width] * (2 * layers) + [units] * layers
                bias, first, sums = [], 0, extra[:, :, 0]
                for size in widths:
                    own = sums[:, :, first : first + size // parts].reshape(teams * parts, -1)
                    column = jnp.arange(size)
                    spread = (
                        jnp.arange(size // parts)[:, None] == (column // HD * per + column % per)[None]
                    ).astype(BF16)
                    mask = (jnp.asarray(places)[:, None] ^ dp_at) == (column % HD // per)[None]
                    full = jnp.where(mask[None], dot_nn(own, spread).reshape(teams, parts, size), 0.0)
                    bias.append(jnp.sum(full, axis=1, keepdims=True))
                    first += size // parts
            for _ in range(steps - 1):
                turn(at + 2)
        qkv, prob, context, normal_one, scale_one, token = attend(
            table, entered, weights[at], bias[2 * layer], bias[2 * layer + 1], vecs[layer, 0], doc_ids, last
        )
        last = (token,)
        if at in coming:
            turn(at + 1)
            turn(at + 2)
            weights[at + 1] = turn(at + 1)
            turn(at + 2)
            weights[at + 2] = turn(at + 2)
        low, active, slope, current, normal_two, scale_two, token = forward(
            table, normal_one, vecs[layer, 0], vecs[layer, 1], bias[2 * layers + layer], weights[at + 1], weights[at + 2], last
        )
        last = (token,)
        saved.append(
            (entered, qkv, prob, context, normal_one, scale_one, low, active, slope, normal_two, scale_two)
        )
    owned, flights, ran, settled = {}, {}, [], ()
    fine = piece % 16 == 0

    def launch(key, grads):
        if key not in SCATTERED:
            flights[key] = scatter_group(*grads, parts)
            next(flights[key])
            return
        if not fine:
            grads = [
                joined(*grads).reshape(teams, parts, piece, -1)[line_of][:, place_of]
                .reshape(teams * model, -1)
            ]
        owned[key] = lax.psum_scatter(
            grads[0], ("tensor", "dp"), scatter_dimension=0, tiled=True
        ).astype(F32)

    def advance(keys, token):
        made = []
        for key in keys:
            got = flights[key].send(token)
            if got.shape != (8, 128):
                owned[key] = got
                del flights[key]
            else:
                made.append(got)
        return tuple(made)

    last = ()

    def push(*keys):
        nonlocal last
        for key in keys:
            if key in flights:
                last = advance([key], last[0] if last else None) or last

    for layer in reversed(range(layers)):
        (entered, qkv, prob, context, normal_one, scale_one, low, active, slope, normal_two, scale_two) = saved[layer]
        *grads, grad_one, sums_two, sums_one, unit_sums, token = forward_back(
            table, upstream, normal_two, scale_two, vecs[layer, 1], active, slope, weights[3 * layer + 1],
            weights[3 * layer + 2], low, normal_one, scale_one, vecs[layer, 0], (layer, 1) in SCATTERED and fine, last,
        )
        last = (token,)
        launch((layer, 1), grads)
        push(*flights)
        *grads, upstream, token = attend_back(
            table, entered, grad_one, weights[3 * layer], qkv, prob, context, unit_sums, sums_one, sums_two, last
        )
        last = (token,)
        launch((layer, 0), grads)
        push(*flights)
    first, second, third, final = list(flights)
    push(first, final, third)
    output = from_sequence(reorder(current, place, last), core)
    push(final, second, third)
    grad_tokens = from_sequence(reorder(upstream, place, last), core)
    push(final, second, third, final)
    while flights:
        push(*list(flights))
    tops = jnp.stack([owned[layer, 0][-EXTRA:] for layer in range(layers)])
    grads = [[owned[layer, 0][:piece], owned[layer, 1][:, :units], owned[layer, 1][:, units:]] for layer in range(layers)]

    qkv_sums = tops[:, 0, : 3 * width].reshape(layers, 3, heads, parts, per)
    qkv_sums = lax.dynamic_index_in_dim(qkv_sums, dp_at, 3, keepdims=False)
    grad_qv = jnp.stack([qkv_sums[:, 0], qkv_sums[:, 2]], axis=1)
    unit_sums = tops[:, 1, :units].reshape(layers, units // HD, parts, per)
    grad_unit = lax.dynamic_index_in_dim(unit_sums, dp_at, 2, keepdims=False)
    row_sums = tops[:, 2:8, :piece].reshape(layers, 2, 3, piece)

    grad_attn = jnp.stack([g[0] for g in grads])
    grad_qkv = jnp.stack(
        [grad_attn[:, :, i * width : (i + 1) * width] for i in range(3)], axis=1
    )
    return (
        output,
        grad_tokens,
        grad_qkv,
        jnp.swapaxes(grad_attn[:, :, 3 * width :], 1, 2),
        jnp.stack([g[1] for g in grads]),
        jnp.swapaxes(jnp.stack([g[2] for g in grads]), 1, 2),
        grad_qv,
        grad_unit,
        row_sums[:, :, 2],
        row_sums[:, :, 0],
        row_sums[:, :, 1],
    )


def solution(mesh):
    placed = (
        P(None, ("dp", "tensor"), None),
        P(None, ("dp", "tensor"), None),
        P(None, "dp", None),
        P(None, None, "dp", "tensor"),
        P(None, "tensor", "dp"),
        P(None, "dp", "tensor"),
        P(None, "tensor", "dp"),
        P(None, None, "tensor", "dp"),
        P(None, "tensor", "dp"),
        P(None, None, "dp"),
        P(None, None, "dp"),
        P(None, None, "dp"),
    )
    return jax.shard_map(
        on_device,
        mesh=mesh,
        in_specs=placed,
        out_specs=(
            P(None, ("dp", "tensor"), None),
            P(None, ("dp", "tensor"), None),
            P(None, None, "dp", "tensor"),
            P(None, "tensor", "dp"),
            P(None, "dp", "tensor"),
            P(None, "tensor", "dp"),
            P(None, None, "tensor", "dp"),
            P(None, "tensor", "dp"),
            P(None, None, "dp"),
            P(None, None, "dp"),
            P(None, None, "dp"),
        ),
        check_vma=False,
    )
```

```python
from functools import partial

import jax
import jax.numpy as jnp
from jax import lax
from jax.experimental import pallas as pl
from jax.experimental.pallas import tpu as pltpu
from jax.sharding import PartitionSpec as P

HD = 64
NORM_EPSILON = 1e-12
MASK_VALUE = -1000000000.0
F32 = jnp.float32
BF16 = jnp.bfloat16
STREAM_BYTES = 60 * 1024 * 1024
MERGE_BYTES = 32 * 1024 * 1024
FORWARD_SCALE, BACKWARD_SCALE = 0.5, 100


def lasting(microseconds, scale):
    return pl.CostEstimate(flops=int(1.15e9 * microseconds * scale), bytes_accessed=0, transcendentals=0)


ROOT_HALF = 0.7071067811865476
ROOT_TWO_PI = 0.3989422804014327

LINE = (1, 3, 0, 2)

GATHERED = (1,)
SCATTERED = ()


def dot_nn(left, right):
    return lax.dot_general(left, right, (((1,), (0,)), ((), ())), preferred_element_type=F32)


def dot_nt(left, right):
    return lax.dot_general(left, right, (((1,), (1,)), ((), ())), preferred_element_type=F32)


def dot_tn(left, right):
    return lax.dot_general(left, right, (((0,), (0,)), ((), ())), preferred_element_type=F32)


def normed_rows(values):
    centre = values - jnp.mean(values, axis=-1, keepdims=True)
    spread = jnp.mean(centre * centre, axis=-1, keepdims=True)
    scale = lax.rsqrt(spread + NORM_EPSILON)
    return centre * scale, scale


def norm_back(upstream, normal, scale, gain):
    grad = upstream * gain
    mean_grad = jnp.mean(grad, axis=-1, keepdims=True)
    mean_both = jnp.mean(grad * normal, axis=-1, keepdims=True)
    return scale * (grad - mean_grad - normal * mean_both)


def token_sums(upstream, normal, result):
    return jnp.concatenate(
        [
            jnp.sum(upstream * normal, axis=0, keepdims=True),
            jnp.sum(upstream, axis=0, keepdims=True),
            jnp.sum(result, axis=0, keepdims=True),
        ],
        axis=0,
    )


def turned(values):
    return values.astype(F32).T.astype(BF16)


ANYWHERE = pl.BlockSpec(memory_space=pl.ANY)
IN_VMEM = pl.BlockSpec(memory_space=pltpu.VMEM)
IN_SMEM = pl.BlockSpec(memory_space=pltpu.SMEM)


def shaped(shape, dtype):
    return jax.ShapeDtypeStruct(tuple(shape), dtype)


class Rows:
    def __init__(self, array, split=False):
        self.operands = [array]
        self.scratch = [
            pltpu.VMEM(array.shape, array.dtype),
            pltpu.SemaphoreType.DMA((array.shape[0] if split else 1,)),
        ]

    def bind(self, refs, scratch, table):
        (self.ref,), (self.held, self.sems) = refs, scratch
        return self

    def copy(self, index):
        if index is None:
            return pltpu.make_async_copy(self.ref, self.held, self.sems.at[0])
        return pltpu.make_async_copy(self.ref.at[index], self.held.at[index], self.sems.at[index])

    def start(self, index=None):
        self.copy(index).start()

    def wait(self, index=None):
        self.copy(index).wait()


class Weights:
    def __init__(self, group, start, width):
        self.group, self.cols = group, pl.ds(group.start + start, width)
        self.operands = list(group.arrays)
        model = group.model
        self.scratch = [
            pltpu.VMEM((len(LINE), model, width), BF16),
            pltpu.SemaphoreType.DMA((len(LINE), len(group.places))),
        ]

    def bind(self, refs, scratch, table):
        self.refs, (self.held, self.sems), self.table = refs, scratch, table
        return self

    def copies(self, index):
        if not self.group.common and self.group.pitch * len(self.group.places) == self.group.model:
            yield pltpu.make_async_copy(
                self.refs[index].at[:, self.cols], self.held.at[index], self.sems.at[index, 0]
            )
            return
        places = len(self.group.places)
        piece = self.group.model // places
        for place in range(places):
            if self.group.common:
                ref = self.refs[0]
                row = pl.multiple_of(self.table[index] + self.table[len(LINE) + place], piece)
            else:
                ref, row = self.refs[index], place * self.group.pitch
            yield pltpu.make_async_copy(
                ref.at[pl.ds(row, piece), self.cols],
                self.held.at[index, pl.ds(place * piece, piece)],
                self.sems.at[index, place],
            )

    def start(self, index):
        for copy in self.copies(index):
            copy.start()

    def wait(self, index):
        for copy in self.copies(index):
            copy.wait()


class Result:
    def __init__(self, shape, dtype, split=False):
        self.shapes = [shaped(shape, dtype)]
        self.indices = range(shape[0]) if split else (None,)
        self.scratch = [
            pltpu.VMEM(shape, dtype),
            pltpu.SemaphoreType.DMA((shape[0] if split else 1,)),
        ]

    def bind(self, refs, scratch, table):
        (self.ref,), (self.held, self.sems) = refs, scratch
        return self

    def copy(self, index):
        if index is None:
            return pltpu.make_async_copy(self.held, self.ref, self.sems.at[0])
        return pltpu.make_async_copy(self.held.at[index], self.ref.at[index], self.sems.at[index])

    def start(self, index=None):
        self.copy(index).start()

    def finish(self):
        for index in self.indices:
            self.copy(index).wait()


class Grads:
    def __init__(self, model, width, places, common):
        self.model, self.places, self.common = model, places, common
        teams = len(LINE)
        if common:
            self.shapes = [shaped((teams * model, width), BF16)]
        else:
            self.shapes = [shaped((2, model, width), BF16)] * 2
        self.scratch = [
            pltpu.VMEM((teams, model, width), BF16),
            pltpu.SemaphoreType.DMA((teams, len(places) if common else 1)),
        ]

    def bind(self, refs, scratch, table):
        self.refs, (self.held, self.sems), self.table = refs, scratch, table
        return self

    def copies(self, index):
        if not self.common:
            yield pltpu.make_async_copy(
                self.held.at[index], self.refs[index // 2].at[index % 2], self.sems.at[index, 0]
            )
            return
        places = len(self.places)
        piece = self.model // places
        for place in range(places):
            row = pl.multiple_of(self.table[index] + self.table[len(LINE) + place], piece)
            yield pltpu.make_async_copy(
                self.held.at[index, pl.ds(place * piece, piece)],
                self.refs[0].at[pl.ds(row, piece)],
                self.sems.at[index, place],
            )

    def start(self, index):
        for copy in self.copies(index):
            copy.start()

    def finish(self):
        for index in range(len(LINE)):
            for copy in self.copies(index):
                copy.wait()


def streamed(body, name, table, ins, outs, scratch=(), after=(), lasts=15, scale=FORWARD_SCALE):
    waits = len(after)
    operands = [array for item in ins for array in item.operands]
    shapes = [shape for item in outs for shape in item.shapes]

    def wrapped(*refs):
        refs = list(refs)

        def take(count):
            taken = refs[:count]
            del refs[:count]
            return taken

        (table_ref,) = take(1)
        in_refs = [take(len(item.operands)) for item in ins]
        take(waits)
        out_refs = [take(len(item.shapes)) for item in outs]
        (token_ref,) = take(1)
        token_ref[...] = jnp.zeros((8, 128), F32)
        inlets = [item.bind(own, take(len(item.scratch)), table_ref) for item, own in zip(ins, in_refs)]
        outlets = [item.bind(own, take(len(item.scratch)), table_ref) for item, own in zip(outs, out_refs)]
        body(inlets, outlets, *refs)
        for outlet in outlets:
            outlet.finish()

    kernel = pl.pallas_call(
        wrapped,
        in_specs=[IN_SMEM] + [ANYWHERE] * (len(operands) + waits),
        out_specs=[ANYWHERE] * len(shapes) + [IN_VMEM],
        out_shape=shapes + [shaped((8, 128), F32)],
        scratch_shapes=[entry for item in list(ins) + list(outs) for entry in item.scratch] + list(scratch),
        compiler_params=pltpu.CompilerParams(vmem_limit_bytes=STREAM_BYTES),
        cost_estimate=lasting(lasts, scale),
        name=name,
    )
    return kernel(table, *operands, *after)


def attend_body(inlets, outlets, low_ref):
    x, doc_col, doc_row, vec, q_bias, v_bias, weights = inlets
    qkv, prob, context, normal_out, scale_out = outlets
    steps, _, width = q_bias.held.shape
    heads = width // HD
    for inlet in (doc_col, doc_row, vec, q_bias, v_bias, x):
        inlet.start()
    weights.start(0)
    for inlet in (doc_col, doc_row, vec, q_bias, v_bias, x):
        inlet.wait()
    low_ref[...] = x.held[...].astype(BF16)
    total = x.held[...].astype(F32) + vec.held[0:1]
    same_doc = doc_col.held[...] == doc_row.held[...]
    for step in range(steps):
        weights.wait(step)
        if step + 1 < steps:
            weights.start(step + 1)
        projected = dot_nn(low_ref[...], weights.held[step, :, : 3 * width])
        queries = (projected[:, :width] + q_bias.held[step]).astype(BF16) * jnp.asarray(0.125, BF16)
        key_rows = projected[:, width : 2 * width].astype(BF16)
        value_full = projected[:, 2 * width :] + v_bias.held[step]
        qkv.held[step, :, :width] = queries
        qkv.held[step, :, width : 2 * width] = key_rows
        qkv.held[step, :, 2 * width :] = value_full.astype(BF16)
        qkv.start(step)
        value_turned = turned(value_full)
        parts = []
        for head in range(heads):
            cols = slice(head * HD, (head + 1) * HD)
            scores = jnp.where(same_doc, dot_nt(key_rows[:, cols], queries[:, cols]), MASK_VALUE)
            expo = jnp.exp(scores - jnp.max(scores, axis=0, keepdims=True))
            chances = (expo * (1.0 / jnp.sum(expo, axis=0, keepdims=True))).astype(BF16)
            prob.held[step * heads + head] = chances
            prob.start(step * heads + head)
            parts.append(dot_nn(value_turned[cols], chances))
        context_turned = jnp.concatenate(parts, axis=0)
        context.held[step] = context_turned.astype(BF16)
        context.start(step)
        total = total + dot_nt(context_turned.T.astype(BF16), weights.held[step, :, 3 * width :])
    normal, scale = normed_rows(total)
    normal_out.held[...] = normal
    scale_out.held[...] = scale
    normal_out.start()
    scale_out.start()


def attend(table, x, weights, q_bias, v_bias, vec, doc_ids, after=()):
    steps, width = q_bias.shape[0], q_bias.shape[2]
    rows, model = x.shape
    heads = width // HD
    return streamed(
        attend_body,
        "attend",
        table,
        [
            Rows(x), Rows(doc_ids.reshape(rows, 1)), Rows(doc_ids.reshape(1, rows)), Rows(vec), Rows(q_bias),
            Rows(v_bias), Weights(weights, 0, 4 * width),
        ],
        [
            Result((steps, rows, 3 * width), BF16, True),
            Result((steps * heads, rows, rows), BF16, True),
            Result((steps, width, rows), BF16, True),
            Result((rows, model), F32),
            Result((rows, 1), F32),
        ],
        [pltpu.VMEM((rows, model), BF16)],
        after=after,
    )


def forward_body(inlets, outlets, low_ref):
    normal, vec, vec_two, bias, first, second = inlets
    low_out, active, slope, out, normal_two, scale_two = outlets
    steps = bias.held.shape[0]
    for inlet in (vec, vec_two, bias, normal):
        inlet.start()
    first.start(0)
    second.start(0)
    for inlet in (vec, vec_two, bias, normal):
        inlet.wait()
    rows = normal.held[...] * vec.held[1:2] + vec.held[2:3]
    low_ref[...] = rows.astype(BF16)
    low_out.held[...] = rows.astype(BF16)
    low_out.start()
    total = rows + vec_two.held[0:1]
    for step in range(steps):
        first.wait(step)
        second.wait(step)
        if step + 1 < steps:
            first.start(step + 1)
            second.start(step + 1)
        hidden = dot_nn(low_ref[...], first.held[step]) + bias.held[step]
        below = 0.5 + 0.5 * lax.erf(hidden * ROOT_HALF)
        value = (hidden * below).astype(BF16)
        active.held[step] = value
        slope.held[step] = (below + hidden * (jnp.exp(hidden * hidden * -0.5) * ROOT_TWO_PI)).astype(BF16)
        active.start(step)
        slope.start(step)
        total = total + dot_nt(value, second.held[step])
    normal_value, scale = normed_rows(total)
    normal_two.held[...] = normal_value
    scale_two.held[...] = scale
    out.held[...] = normal_value * vec_two.held[1:2] + vec_two.held[2:3]
    for outlet in (normal_two, scale_two, out):
        outlet.start()


def forward(table, normal, vec, vec_two, bias, first, second, after=()):
    steps, _, width = bias.shape
    rows, model = normal.shape
    return streamed(
        forward_body,
        "forward",
        table,
        [
            Rows(normal), Rows(vec), Rows(vec_two), Rows(bias),
            Weights(first, 0, width), Weights(second, 0, width),
        ],
        [
            Result((rows, model), BF16),
            Result((steps, rows, width), BF16, True),
            Result((steps, rows, width), BF16, True),
            Result((rows, model), F32),
            Result((rows, model), F32),
            Result((rows, 1), F32),
        ],
        [pltpu.VMEM((rows, model), BF16)],
        after=after,
    )


def forward_back_body(inlets, outlets, low_two_ref):
    up, normal_two, scale_two, vec_two, active, slope, second, first, low, normal, scale, vec = inlets
    grads, grad_one, sums_two, sums_one, unit_sums = outlets
    steps, _, width = active.held.shape
    for inlet in (scale_two, vec_two, up, normal_two):
        inlet.start()
    for inlet in (scale_two, vec_two, up, normal_two):
        inlet.wait()

    def bring(step):
        for inlet in (active, second, slope, first):
            inlet.start(step)

    bring(0)
    low.start()
    upstream, normal_value = up.held[...].astype(F32), normal_two.held[...]
    grad = norm_back(upstream, normal_value, scale_two.held[...], vec_two.held[1:2])
    low_two_ref[...] = grad.astype(BF16)
    total = grad
    sums_two.held[...] = token_sums(upstream, normal_value, grad)
    sums_two.start()
    for step in range(steps):
        for inlet in (active, second, slope, first):
            inlet.wait(step)
        if step == 0:
            low.wait()
        if step + 1 < steps:
            bring(step + 1)
        if step + 2 == steps:
            for inlet in (scale, vec, normal):
                inlet.start()
        grads.held[step, :, width:] = dot_tn(low_two_ref[...], active.held[step]).astype(BF16)
        value = (dot_nn(low_two_ref[...], second.held[step]) * slope.held[step].astype(F32)).astype(BF16)
        unit_sums.held[step] = jnp.sum(value.astype(F32), axis=0, keepdims=True)
        grads.held[step, :, :width] = dot_tn(low.held[...], value).astype(BF16)
        grads.start(step)
        unit_sums.start(step)
        total = total + dot_nt(value, first.held[step])
    for inlet in (scale, vec, normal):
        inlet.wait()
    normal_value = normal.held[...]
    grad = norm_back(total, normal_value, scale.held[...], vec.held[1:2])
    grad_one.held[...] = grad
    sums_one.held[...] = token_sums(total, normal_value, grad)
    grad_one.start()
    sums_one.start()


def forward_back(
    table, upstream, normal_two, scale_two, vec_two, active, slope, first, second, low, normal, scale, vec, common,
    after=(),
):
    steps, rows, width = active.shape
    model = low.shape[1]
    return streamed(
        forward_back_body,
        "forward_back",
        table,
        [
            Rows(upstream), Rows(normal_two), Rows(scale_two), Rows(vec_two), Rows(active, True), Rows(slope, True),
            Weights(second, 0, width), Weights(first, 0, width), Rows(low), Rows(normal), Rows(scale), Rows(vec),
        ],
        [
            Grads(model, 2 * width, first.places, common),
            Result((rows, model), F32),
            Result((3, model), F32),
            Result((3, model), F32),
            Result((steps, 1, width), F32, True),
        ],
        [pltpu.VMEM((rows, model), BF16)],
        after=after,
        lasts=19,
        scale=BACKWARD_SCALE,
    )


def attend_back_body(inlets, outlets, low_ref, x_low_ref):
    x, grad_one, qkv, prob, context, weights, unit_sums, sums_one, sums_two = inlets
    grads, grad_x = outlets
    places = len(grads.places)
    model = x.held.shape[1]
    piece, pitch = model // places, grads.held.shape[1] // places
    steps, width, _ = context.held.shape
    heads = prob.held.shape[0] // steps

    def bring(step):
        weights.start(step)
        qkv.start(step)
        for head in range(heads):
            prob.start(step * heads + head)
        context.start(step)

    grad_one.start()
    bring(0)
    x.start()
    for inlet in (unit_sums, sums_one, sums_two):
        inlet.start()
    grad_one.wait()
    low_ref[...] = grad_one.held[...].astype(BF16)
    total = grad_one.held[...]
    for inlet in (unit_sums, sums_one, sums_two):
        inlet.wait()
    sums = jnp.concatenate([sums_one.held[...], sums_two.held[...]], axis=0)
    for step in range(steps):
        weights.wait(step)
        qkv.wait(step)
        context.wait(step)
        for head in range(heads):
            prob.wait(step * heads + head)
        if step == 0:
            x.wait()
            x_low_ref[...] = x.held[...].astype(BF16)
        if step + 1 < steps:
            bring(step + 1)
        block = qkv.held[step]
        queries, key_rows = block[:, :width], block[:, width : 2 * width]
        value_rows = block[:, 2 * width :]
        key_turned = turned(key_rows)
        grad_context = dot_nn(low_ref[...], weights.held[step, :, 3 * width :]).astype(BF16)
        grad_q, grad_k, grad_v = [], [], []
        for head in range(heads):
            cols = slice(head * HD, (head + 1) * HD)
            low_weights = prob.held[step * heads + head]
            chances = low_weights.astype(F32)
            part = chances * dot_nt(value_rows[:, cols], grad_context[:, cols])
            centre = jnp.sum(part, axis=0, keepdims=True)
            grad_scores = (part - chances * centre).astype(BF16)
            grad_v.append(dot_nn(low_weights, grad_context[:, cols]))
            grad_k.append(dot_nn(grad_scores, queries[:, cols]))
            grad_q.append(dot_nn(key_turned[cols], grad_scores))
        stacked = jnp.concatenate(
            [(jnp.concatenate(grad_q, axis=0) * 0.125).T] + grad_k + grad_v, axis=1
        ).astype(BF16)
        qkv_grad = dot_tn(x_low_ref[...], stacked)
        out_grad = dot_tn(low_ref[...], turned(context.held[step]))
        qkv_sums = jnp.sum(stacked.astype(F32), axis=0, keepdims=True)
        top = jnp.concatenate(
            [jnp.concatenate([qkv_sums, jnp.zeros((1, width), F32)], axis=1), unit_sums.held[step]], axis=0
        )
        for place in range(places):
            rows = slice(place * piece, (place + 1) * piece)
            at = place * pitch
            grads.held[step, at : at + piece, : 3 * width] = qkv_grad[rows].astype(BF16)
            grads.held[step, at : at + piece, 3 * width :] = out_grad[rows].astype(BF16)
            own = jnp.concatenate([sums[:, rows], jnp.zeros((6, 4 * width - piece), F32)], axis=1)
            grads.held[step, at + pitch - EXTRA : at + pitch] = jnp.concatenate(
                [top, own, jnp.zeros((EXTRA - 8, 4 * width), F32)], axis=0
            ).astype(BF16)
        grads.start(step)
        total = total + dot_nt(stacked, weights.held[step, :, : 3 * width])
    grad_x.held[...] = total
    grad_x.start()


def attend_back(
    table, x, grad_one, weights, qkv, prob, context, unit_sums, sums_one, sums_two, after=()
):
    steps, width, rows = context.shape
    model = x.shape[1]
    return streamed(
        attend_back_body,
        "attend_back",
        table,
        [
            Rows(x), Rows(grad_one), Rows(qkv, True), Rows(prob, True), Rows(context, True),
            Weights(weights, 0, 4 * width), Rows(unit_sums), Rows(sums_one), Rows(sums_two),
        ],
        [
            Grads(len(weights.places) * (-(-model // len(weights.places) // 16) * 16 + EXTRA), 4 * width, weights.places, False),
            Result((rows, model), F32),
        ],
        [pltpu.VMEM((rows, model), BF16), pltpu.VMEM((rows, model), BF16)],
        after=after,
        lasts=22,
        scale=BACKWARD_SCALE,
    )


def whole(shape):
    return pl.BlockSpec(shape, lambda t: (0,) * len(shape))


def call(body, name, steps, in_specs, out_specs, out_shape, scratch, flops, moved, after=(), token=False):
    single = not isinstance(out_shape, list)
    out_specs = [out_specs] if single else list(out_specs)
    out_shape = [out_shape] if single else list(out_shape)
    inputs, outputs, waits = len(in_specs), len(out_shape), len(after)
    if token:
        out_specs.append(whole((8, 128)))
        out_shape.append(shaped((8, 128), F32))

    def wrapped(*refs):
        made = refs[inputs + waits :]
        if token:
            made[outputs][...] = jnp.zeros((8, 128), F32)
        body(*refs[:inputs], *made[:outputs], *made[outputs + token :])

    kernel = pl.pallas_call(
        wrapped,
        grid=(steps,),
        in_specs=list(in_specs) + [ANYWHERE] * waits,
        out_specs=out_specs,
        out_shape=out_shape,
        scratch_shapes=scratch,
        compiler_params=pltpu.CompilerParams(
            dimension_semantics=("arbitrary",), vmem_limit_bytes=MERGE_BYTES
        ),
        cost_estimate=lasting(2, BACKWARD_SCALE),
        name=name,
    )

    def run(*args):
        made = kernel(*args, *after)
        if not single or token:
            return made
        return made[0]

    return run


def reorder_kernel(values_ref, place_ref, out_ref):
    values = values_ref[...]
    high = values.astype(BF16)
    low = (values - high.astype(F32)).astype(BF16)
    place = place_ref[...]
    out_ref[...] = dot_nt(high, place) + dot_nt(low, place)


def reorder(values, place, after=()):
    rows, model = values.shape
    return call(
        reorder_kernel,
        "reorder",
        1,
        [whole((rows, model)), whole((model, model))],
        whole((rows, model)),
        shaped((rows, model), F32),
        [],
        4 * rows * model * model,
        8 * rows * model,
        after=after,
    )(values, place)


def dp_bits(parts):
    return list(range(1, parts.bit_length() - 1))[::-1] + [0]


def dp_places(parts):
    bits = dp_bits(parts)
    return [sum(((place >> k) & 1) << bit for k, bit in enumerate(bits)) for place in range(parts)]


def trade(values, axis, bit):
    return lax.ppermute(values, axis, [(i, i ^ (1 << bit)) for i in range(lax.axis_size(axis))])


def swap_cores(values):
    return trade(values, "tensor", 0)


def to_sequence(blocks, core):
    mine = lax.dynamic_index_in_dim(blocks, core, 0, keepdims=False)
    other = lax.dynamic_index_in_dim(blocks, 1 - core, 0, keepdims=False)
    got = swap_cores(other)
    return jnp.concatenate(
        [jnp.where(core == 0, mine, got), jnp.where(core == 0, got, mine)], axis=0
    )


def from_sequence(values, core):
    half = values.shape[0] // 2
    mine = lax.dynamic_slice_in_dim(values, core * half, half, 0)
    got = swap_cores(lax.dynamic_slice_in_dim(values, (1 - core) * half, half, 0))
    return jnp.stack([jnp.where(core == 0, mine, got), jnp.where(core == 0, got, mine)])


def joined(*blocks):
    return jnp.concatenate(blocks, axis=0)


def gated(values, token):
    return values if token is None else values + token[0, 0].astype(values.dtype)


class Group:
    def __init__(self, arrays, model, places, common):
        self.arrays, self.model, self.places, self.common = arrays, model, places, common
        self.start, self.pitch = 0, model // len(places)


def mark(*arrays):
    def body(*refs):
        refs[-1][...] = jnp.zeros((8, 128), F32)

    return pl.pallas_call(
        body,
        in_specs=[ANYWHERE] * len(arrays),
        out_specs=IN_VMEM,
        out_shape=shaped((8, 128), F32),
        cost_estimate=lasting(0.5, FORWARD_SCALE),
        name="mark",
    )(*arrays)


def moved(plan, after):
    arrays = []
    for parts in plan:
        for array, _, _ in parts:
            if not any(array is other for other in arrays):
                arrays.append(array)
    steps = []
    for out, parts in enumerate(plan):
        at = 0
        for array, start, rows in parts:
            source = [array is other for other in arrays].index(True)
            steps.append((source, start, out, at, rows))
            at += rows
    shapes = [
        shaped((sum(rows for _, _, rows in parts),) + parts[0][0].shape[1:], parts[0][0].dtype) for parts in plan
    ]
    count, waits = len(arrays), len(after)

    def body(*refs):
        refs = list(refs)
        sources, results = refs[:count], refs[count + waits : count + waits + len(plan)]
        token_ref, *held = refs[count + waits + len(plan) : -2]
        sems, out_sems = refs[-2:]
        token_ref[...] = jnp.zeros((8, 128), F32)
        brought = [
            pltpu.make_async_copy(
                sources[source].at[pl.ds(start, rows)], held[out].at[pl.ds(at, rows)], sems.at[k]
            )
            for k, (source, start, out, at, rows) in enumerate(steps)
        ]
        for copy in brought:
            copy.start()
        for copy in brought:
            copy.wait()
        given = [pltpu.make_async_copy(held[k], results[k], out_sems.at[k]) for k in range(len(plan))]
        for copy in given:
            copy.start()
        for copy in given:
            copy.wait()

    return pl.pallas_call(
        body,
        in_specs=[ANYWHERE] * (count + waits),
        out_specs=[ANYWHERE] * len(shapes) + [IN_VMEM],
        out_shape=shapes + [shaped((8, 128), F32)],
        scratch_shapes=[pltpu.VMEM(shape.shape, shape.dtype) for shape in shapes]
        + [pltpu.SemaphoreType.DMA((len(steps),)), pltpu.SemaphoreType.DMA((len(plan),))],
        compiler_params=pltpu.CompilerParams(vmem_limit_bytes=MERGE_BYTES),
        cost_estimate=lasting(2, FORWARD_SCALE),
        name="moved",
    )(*arrays, *after)


def built(plan, after, fine):
    if fine:
        *made, token = moved(plan, after)
        return made, token
    token = mark(*after) if after else None
    made = [joined(*[gated(array[start : start + rows], token) for array, start, rows in parts]) for parts in plan]
    return made, mark(*made)


def gather_group(shard, places):
    parts = len(places)
    bits = dp_bits(parts)
    fine = shard.shape[0] % 16 == 0
    block = shard
    for bit in bits[:-1]:
        got = trade(block, "dp", bit)
        after = yield None
        rows = block.shape[0]
        (block,), token = built([[(block, 0, rows), (got, 0, rows)]], after, fine)
        yield token
    half = block.shape[0] // 2
    beyond = trade(block, "dp", bits[-1])
    across = trade(block, "tensor", 1)
    after = yield None
    (low, high), token = built([[(across, 0, half)], [(beyond, half, half)]], after, fine)
    yield token
    far_low = trade(low, "dp", bits[-1])
    far_high = trade(high, "tensor", 1)
    after = yield None
    (mine, across), token = built(
        [[(block, 0, 2 * half), (beyond, 0, 2 * half)], [(across, 0, 2 * half), (far_low, 0, half), (far_high, 0, half)]],
        after, fine,
    )
    yield token
    yield Group([swap_cores(mine), swap_cores(across), mine, across], mine.shape[0], places, False)


EXTRA = 16


def padded(rows, to):
    return jnp.pad(rows, ((0, to - rows.shape[0]), (0, 0)))


def without_extra(group, piece):
    parts = len(group.places)
    pitch = group.model // parts
    blocks = [array.reshape(parts, pitch, -1) for array in group.arrays]
    extra = jnp.stack([block[:, pitch - EXTRA :] for block in blocks])
    group.model = parts * piece
    if piece % 16:
        group.arrays = [block[:, :piece].reshape(parts * piece, -1) for block in blocks]
        pitch = piece
    group.pitch = pitch
    return group, extra


def gather_common(shards, places, place_rows):
    parts = len(places)
    piece = shards[0].shape[0]
    model = parts * piece
    got = lax.all_gather(jnp.concatenate(shards, axis=1), ("tensor", "dp"), axis=0, tiled=True)
    groups, start = [], 0
    for shard in shards:
        width = shard.shape[1]
        if piece % 16:
            own = got[:, start : start + width].reshape(len(LINE), parts, piece, width)
            own = own[place_rows[0]][:, place_rows[1]].reshape(len(LINE), model, width)
            groups.append(Group([own[i] for i in range(len(LINE))], model, places, False))
        else:
            groups.append(Group([got], model, places, True))
            groups[-1].start = start
        start += width
    return groups


def added(left, right):
    return left.astype(F32) + right.astype(F32)


def merge_core_kernel(keep_ref, got_ref, across_ref, mine_a_ref, beyond_ref, mine_b_ref):
    total = added(keep_ref[...], got_ref[...]).astype(BF16)

    @pl.when(pl.program_id(0) == 0)
    def _():
        across_ref[...] = total[1]
        mine_a_ref[...] = total[0]

    @pl.when(pl.program_id(0) == 1)
    def _():
        beyond_ref[...] = total[:, 1]
        mine_b_ref[...] = total[:, 0]


def merge_core(keep, got, token):
    _, rows, width = keep.shape
    fourth = rows // 4
    view = (2, 2, 2, fourth, width)
    spec = pl.BlockSpec((2, 2, None, fourth, width), lambda t: (0, 0, t, 0, 0))
    return call(
        merge_core_kernel,
        "merge_core",
        2,
        [spec, spec],
        [whole((2, fourth, width))] * 4,
        [shaped((2, fourth, width), BF16)] * 4,
        [],
        keep.size,
        keep.size * 6,
        after=() if token is None else (token,),
        token=True,
    )(keep.reshape(view), got.reshape(view))


def merge_sides_kernel(a_ref, got_a_ref, b_ref, got_b_ref, keep_a_ref, send_a_ref, keep_b_ref, send_b_ref):
    keep_a_ref[...] = added(a_ref[0], got_a_ref[0]).astype(BF16)
    send_a_ref[...] = added(a_ref[1], got_a_ref[1]).astype(BF16)
    keep_b_ref[...] = added(b_ref[0], got_b_ref[0]).astype(BF16)
    send_b_ref[...] = added(b_ref[1], got_b_ref[1]).astype(BF16)


def merge_sides(a, got_a, b, got_b, token):
    _, rows, width = a.shape
    return call(
        merge_sides_kernel,
        "merge_sides",
        1,
        [whole((2, rows, width))] * 4,
        [whole((rows, width))] * 4,
        [shaped((rows, width), BF16)] * 4,
        [],
        a.size,
        a.size * 12,
        after=() if token is None else (token,),
        token=True,
    )(a, got_a, b, got_b)


def merge_pair_kernel(a_ref, got_a_ref, b_ref, got_b_ref, out_a_ref, out_b_ref):
    out_a_ref[...] = added(a_ref[...], got_a_ref[...]).astype(BF16)
    out_b_ref[...] = added(b_ref[...], got_b_ref[...]).astype(BF16)


def merge_pair(a, got_a, b, got_b, token):
    rows, width = a.shape
    return call(
        merge_pair_kernel,
        "merge_pair",
        1,
        [whole((rows, width))] * 4,
        [whole((rows, width))] * 2,
        [shaped((rows, width), BF16)] * 2,
        [],
        a.size,
        a.size * 12,
        after=() if token is None else (token,),
        token=True,
    )(a, got_a, b, got_b)


def merge_halves_kernel(a_ref, got_ref, keep_ref, send_ref):
    half = keep_ref.shape[0]
    keep_ref[...] = added(a_ref[:half], got_ref[:half]).astype(BF16)
    send_ref[...] = added(a_ref[half:], got_ref[half:]).astype(BF16)


def merge_halves(a, got, token):
    rows, width = a.shape
    return call(
        merge_halves_kernel,
        "merge_halves",
        1,
        [whole((rows, width))] * 2,
        [whole((rows // 2, width))] * 2,
        [shaped((rows // 2, width), BF16)] * 2,
        [],
        a.size,
        a.size * 6,
        after=() if token is None else (token,),
        token=True,
    )(a, got)


def scatter_group(send, keep, parts):
    bits = dp_bits(parts)
    got = swap_cores(send)
    token = yield None
    across, mine_a, beyond, mine_b, ran = merge_core(keep, got, token)
    got_a, got_b = trade(across, "tensor", 1), trade(beyond, "dp", bits[-1])
    token = yield ran
    keep_a, send_a, keep_b, send_b, ran = merge_sides(mine_a, got_a, mine_b, got_b, token)
    got_a, got_b = trade(send_a, "dp", bits[-1]), trade(send_b, "tensor", 1)
    token = yield ran
    keep, send, ran = merge_pair(keep_a, got_a, keep_b, got_b, token)
    for bit in reversed(bits[1:-1]):
        got = trade(send, "dp", bit)
        token = yield ran
        keep, send, ran = merge_halves(keep, got, token)
    got = trade(send, "dp", bits[0])
    token = yield ran
    yield added(keep, gated(got, token))


def on_device(
    tokens, cotangent, segment_ids, qkv_weight, out_weight, in_weight, down_weight,
    qv_bias, in_bias, row_bias, norm_gain, norm_shift,
):
    teams, parts = lax.axis_size("tensor"), lax.axis_size("dp")
    layers, _, piece, width = qkv_weight.shape
    heads = width // HD
    model = piece * parts
    units = in_weight.shape[2]
    tensor_at, dp_at = lax.axis_index("tensor"), lax.axis_index("dp")
    core = tensor_at % 2

    places = dp_places(parts)
    column = jnp.arange(model)
    source = (jnp.asarray(places)[column // piece] ^ dp_at) * piece + column % piece
    place = (column[:, None] == source[None, :]).astype(BF16)

    starts = (jnp.asarray(LINE) ^ tensor_at) * model
    rows = (jnp.asarray(places) ^ dp_at) * piece
    table = jnp.concatenate([starts, rows]).astype(jnp.int32)
    from_common = (jnp.asarray(LINE) ^ tensor_at, jnp.asarray(places) ^ dp_at)

    out_turned = jnp.swapaxes(out_weight, 1, 2)
    down_turned = jnp.swapaxes(down_weight, 1, 2)
    shards = []
    for layer in range(layers):
        shards.append(
            jnp.concatenate([qkv_weight[layer, i] for i in range(3)] + [out_turned[layer]], axis=1)
        )
        shards += [in_weight[layer], down_turned[layer]]

    doc_ids = segment_ids[core, tensor_at // 2]
    current = dot_nn(to_sequence(tokens, core), place).astype(BF16)
    upstream = dot_nn(to_sequence(cotangent, core), place).astype(BF16)

    per = HD // parts
    lanes = [qv_bias[layer, i].reshape(-1) for layer in range(layers) for i in range(2)]
    lanes += [in_bias[layer].reshape(-1) for layer in range(layers)]
    lanes = jnp.concatenate(lanes)
    wide = shards[0].shape[1]
    vectors = jnp.stack([row_bias, norm_gain, norm_shift], axis=2).reshape(-1, piece)
    extra = jnp.concatenate(
        [jnp.pad(lanes, (0, wide - lanes.size))[None], jnp.pad(vectors, ((0, 0), (0, wide - piece)))]
    )
    filled = -(-piece // 16) * 16
    shards[0] = joined(padded(shards[0], filled), padded(extra, EXTRA))

    coming = {at: gather_group(shard, places) for at, shard in enumerate(shards) if at // 3 not in GATHERED}
    for group in coming.values():
        next(group)
    steps = len(dp_bits(parts)) - 1
    last = ()

    def turn(index, after=()):
        nonlocal last
        last = (coming[index].send(tuple(last) + tuple(after)),)
        return next(coming[index])

    for _ in range(steps):
        turn(0)
    weights = {}
    for layer in GATHERED:
        own = [gated(shard, last[0]) for shard in shards[3 * layer : 3 * layer + 3]]
        for kind, group in enumerate(gather_common(own, places, from_common)):
            weights[3 * layer + kind] = group

    ready = (current, upstream)
    saved = []
    for layer in range(layers):
        at = 3 * layer
        entered = current
        if at in coming:
            for _ in range(steps if at else 0):
                turn(at)
            for _ in range(steps - 1):
                turn(at + 1)
            turn(at, ready)
            turn(at + 1)
            weights[at] = turn(at)
            if at == 0:
                weights[0], extra = without_extra(weights[0], piece)
                vecs = (
                    extra[0, :, 1 : 1 + 6 * layers, :piece].transpose(1, 0, 2)
                    .reshape(layers, 2, 3, model).astype(F32)
                )
                widths = [width] * (2 * layers) + [units] * layers
                bias, first, sums = [], 0, extra[:, :, 0]
                for size in widths:
                    own = sums[:, :, first : first + size // parts].reshape(teams * parts, -1)
                    column = jnp.arange(size)
                    spread = (
                        jnp.arange(size // parts)[:, None] == (column // HD * per + column % per)[None]
                    ).astype(BF16)
                    mask = (jnp.asarray(places)[:, None] ^ dp_at) == (column % HD // per)[None]
                    full = jnp.where(mask[None], dot_nn(own, spread).reshape(teams, parts, size), 0.0)
                    bias.append(jnp.sum(full, axis=1, keepdims=True))
                    first += size // parts
            for _ in range(steps - 1):
                turn(at + 2)
        qkv, prob, context, normal_one, scale_one, token = attend(
            table, entered, weights[at], bias[2 * layer], bias[2 * layer + 1], vecs[layer, 0], doc_ids, last
        )
        last = (token,)
        if at in coming:
            turn(at + 1)
            turn(at + 2)
            weights[at + 1] = turn(at + 1)
            turn(at + 2)
            weights[at + 2] = turn(at + 2)
        low, active, slope, current, normal_two, scale_two, token = forward(
            table, normal_one, vecs[layer, 0], vecs[layer, 1], bias[2 * layers + layer], weights[at + 1], weights[at + 2], last
        )
        last = (token,)
        saved.append(
            (entered, qkv, prob, context, normal_one, scale_one, low, active, slope, normal_two, scale_two)
        )
    owned, flights, ran, settled = {}, {}, [], ()
    fine = piece % 16 == 0

    def launch(key, grads):
        if key not in SCATTERED:
            flights[key] = scatter_group(*grads, parts)
            next(flights[key])
            return
        if not fine:
            grads = [
                joined(*grads).reshape(teams, parts, piece, -1)[line_of][:, place_of]
                .reshape(teams * model, -1)
            ]
        owned[key] = lax.psum_scatter(
            grads[0], ("tensor", "dp"), scatter_dimension=0, tiled=True
        ).astype(F32)

    def advance(keys, token):
        made = []
        for key in keys:
            got = flights[key].send(token)
            if got.shape != (8, 128):
                owned[key] = got
                del flights[key]
            else:
                made.append(got)
        return tuple(made)

    last = ()

    def push(*keys):
        nonlocal last
        for key in keys:
            if key in flights:
                last = advance([key], last[0] if last else None) or last

    for layer in reversed(range(layers)):
        (entered, qkv, prob, context, normal_one, scale_one, low, active, slope, normal_two, scale_two) = saved[layer]
        *grads, grad_one, sums_two, sums_one, unit_sums, token = forward_back(
            table, upstream, normal_two, scale_two, vecs[layer, 1], active, slope, weights[3 * layer + 1],
            weights[3 * layer + 2], low, normal_one, scale_one, vecs[layer, 0], (layer, 1) in SCATTERED and fine, last,
        )
        last = (token,)
        launch((layer, 1), grads)
        push(*flights)
        *grads, upstream, token = attend_back(
            table, entered, grad_one, weights[3 * layer], qkv, prob, context, unit_sums, sums_one, sums_two, last
        )
        last = (token,)
        launch((layer, 0), grads)
        push(*flights)
    first, second, third, final = list(flights)
    push(first, second, final, third)
    grad_tokens = from_sequence(reorder(upstream, place, last), core)
    push(final, second, third)
    output = from_sequence(reorder(current, place, last), core)
    push(final)
    while flights:
        push(*list(flights))
    tops = jnp.stack([owned[layer, 0][-EXTRA:] for layer in range(layers)])
    grads = [[owned[layer, 0][:piece], owned[layer, 1][:, :units], owned[layer, 1][:, units:]] for layer in range(layers)]

    qkv_sums = tops[:, 0, : 3 * width].reshape(layers, 3, heads, parts, per)
    qkv_sums = lax.dynamic_index_in_dim(qkv_sums, dp_at, 3, keepdims=False)
    grad_qv = jnp.stack([qkv_sums[:, 0], qkv_sums[:, 2]], axis=1)
    unit_sums = tops[:, 1, :units].reshape(layers, units // HD, parts, per)
    grad_unit = lax.dynamic_index_in_dim(unit_sums, dp_at, 2, keepdims=False)
    row_sums = tops[:, 2:8, :piece].reshape(layers, 2, 3, piece)

    grad_attn = jnp.stack([g[0] for g in grads])
    grad_qkv = jnp.stack(
        [grad_attn[:, :, i * width : (i + 1) * width] for i in range(3)], axis=1
    )
    return (
        output,
        grad_tokens,
        grad_qkv,
        jnp.swapaxes(grad_attn[:, :, 3 * width :], 1, 2),
        jnp.stack([g[1] for g in grads]),
        jnp.swapaxes(jnp.stack([g[2] for g in grads]), 1, 2),
        grad_qv,
        grad_unit,
        row_sums[:, :, 2],
        row_sums[:, :, 0],
        row_sums[:, :, 1],
    )


def solution(mesh):
    placed = (
        P(None, ("dp", "tensor"), None),
        P(None, ("dp", "tensor"), None),
        P(None, "dp", None),
        P(None, None, "dp", "tensor"),
        P(None, "tensor", "dp"),
        P(None, "dp", "tensor"),
        P(None, "tensor", "dp"),
        P(None, None, "tensor", "dp"),
        P(None, "tensor", "dp"),
        P(None, None, "dp"),
        P(None, None, "dp"),
        P(None, None, "dp"),
    )
    return jax.shard_map(
        on_device,
        mesh=mesh,
        in_specs=placed,
        out_specs=(
            P(None, ("dp", "tensor"), None),
            P(None, ("dp", "tensor"), None),
            P(None, None, "dp", "tensor"),
            P(None, "tensor", "dp"),
            P(None, "dp", "tensor"),
            P(None, "tensor", "dp"),
            P(None, None, "tensor", "dp"),
            P(None, "tensor", "dp"),
            P(None, None, "dp"),
            P(None, None, "dp"),
            P(None, None, "dp"),
        ),
        check_vma=False,
    )
```
